128 devices in a mesh: gx: 8 (over x, core), gy: 16 (over z, y).
Axes of the slice: x: 4, y: 4, z: 4, core: 2. Of those that a mesh axis runs over, the one named last changes fastest.
Arguments:
- equation_misfit: float32 [3, 16, 512, 2048], P(None, None, 'gx', 'gy'), may hold values from -6 to 6
- thermal_excess: float32 [16, 512, 2048], P(None, 'gx', 'gy'), may hold values from 0.5 to 1.5
- spanning_vectors: bfloat16 [8, 3, 16, 512, 2048], P(None, None, None, 'gx', 'gy'), may hold values from -6 to 6
- global_solve_pieces: float32 [32, 16, 9, 8, 8], P('gx', 'gy'), may hold values from -0.0009765625 to 0.0009765625
- influencing_partition_table: int32 [32, 16, 9], P('gx', 'gy'), may hold values from 0 to 511, as said below
- spanning_vector_tally: int32 [32, 16], P('gx', 'gy'), may hold values from 1 to 8
Outputs:
- preconditioned: float32 [3, 16, 512, 2048], P(None, None, 'gx', 'gy')
The draws below stay inside these ranges and needn't reach their ends.
Inputs may be any that keep to these rules, and one draw needn't show every extreme that they name: `influencing_partition_table`: entries are subdomain numbers i * 16 + j.
All inputs are finite; a program needn't handle non-finite values.
Results may differ from the reference program's by a relative error of at most 0.0065.
Values sent between devices are 32-bit elements; how exact they have to be, the bound alone decides.
A program may use at most 192 MiB of HBM per device.

```python
import jax
import jax.numpy as jnp
from jax import lax

CY = 128
VERTICAL_LAYERS = 16
OV = 8
SWEEPS = 2
KMAX = 8
NLIST = 9
SX = 16
MESH_NORTHWARD = 512
MESH_EASTWARD = 2048
SUBX = 32
SUBY = 16


def draw_influencing_partition_table(key, part):
    key_rows, key_cols, key_far = jax.random.split(jax.random.fold_in(key, 7), 3)
    shape_all = (SUBX, SUBY, NLIST)
    rows_now = jnp.arange(SUBX)[:, None, None]
    cols_now = jnp.arange(SUBY)[None, :, None]
    step_rows = jax.random.randint(key_rows, shape_all, -2, 3)
    step_cols = jax.random.randint(key_cols, shape_all, -2, 3)
    near_ids = (rows_now + step_rows) % SUBX * SUBY + (cols_now + step_cols) % SUBY
    far_ids = jax.random.randint(key_far, shape_all, 0, SUBX * SUBY)
    lane_ids = jnp.arange(NLIST)[None, None, :]
    chosen = jnp.where(lane_ids < NLIST - 2, near_ids, far_ids)
    chosen = chosen.at[0, 0, NLIST - 1].set(SUBX * SUBY - 1).at[0, 0, NLIST - 2].set(0)
    return chosen.astype(jnp.int32)


def draw_spanning_vector_tally(key, part):
    drawn_counts = jax.random.randint(jax.random.fold_in(key, 5), (SUBX, SUBY), 1, KMAX + 1)
    drawn_counts = drawn_counts.at[0, 0].set(KMAX).at[SUBX - 1, SUBY - 1].set(1)
    return drawn_counts.astype(jnp.int32)


def level_of(own_key, extent, shards, smallest, top_value):
    loudness, own = 1.0, jax.random.fold_in(own_key, 6)
    for dim, blocks in shards:
        heights = jnp.exp(jax.random.uniform(jax.random.fold_in(own, dim), (blocks,), jnp.float32, smallest / len(shards), top_value / len(shards)))
        loudness = loudness * jnp.repeat(heights, extent[dim] // blocks).reshape([-1 if axis == dim else 1 for axis in range(len(extent))])
    return loudness


def noise(own_key, dims, deviation, bound, shards=(), held_as=jnp.bfloat16):
    gain = level_of(own_key, dims, shards, -0.22, 0.18) if shards else 1.0
    values = jax.random.normal(own_key, dims, jnp.float32) * deviation * gain
    return jnp.minimum(jnp.maximum(values, -bound), bound).astype(held_as)


def setup_inputs(seed: int = 0) -> dict:
    splits = jax.random.split(jax.random.key(seed), 7)
    return {
        "equation_misfit": noise(splits[0], (3, VERTICAL_LAYERS, MESH_NORTHWARD, MESH_EASTWARD), 1.0, 6.0, ((2, 8), (3, 16)), jnp.float32),
        "thermal_excess": jnp.clip(0.5 + 1.0 * jax.random.uniform(splits[1], (VERTICAL_LAYERS, MESH_NORTHWARD, MESH_EASTWARD), jnp.float32) ** level_of(splits[1], (VERTICAL_LAYERS, MESH_NORTHWARD, MESH_EASTWARD), ((1, 8), (2, 16)), -0.2, 0.2), 0.5, 1.5),
        "spanning_vectors": noise(splits[2], (KMAX, 3, VERTICAL_LAYERS, MESH_NORTHWARD, MESH_EASTWARD), 1.0, 6.0, ((3, 8), (4, 16))),
        "global_solve_pieces": noise(splits[3], (SUBX, SUBY, NLIST, KMAX, KMAX), (0.2 / (NLIST * KMAX * 3 * VERTICAL_LAYERS * SX * CY) ** 0.5), 0.0009765625, ((0, 8), (1, 16)), jnp.float32),
        "influencing_partition_table": draw_influencing_partition_table(jax.random.fold_in(splits[6], 71), 0),
        "spanning_vector_tally": draw_spanning_vector_tally(jax.random.fold_in(splits[6], 71), 0),
    }


MASS_TERM = 0.05
RELAX_WEIGHT = 0.8
ARRHENIUS_FACTOR = 6.0


def rigidity_magnitude(thermal_excess):
    return 1.0 / (1.0 + jnp.exp(ARRHENIUS_FACTOR * (1.0 - 1.0 / thermal_excess)))


def unity_weights(length):
    position = jnp.arange(length)
    inside = (position >= 2 * OV) & (position < length - 2 * OV)
    return jnp.where(inside, 1.0, 0.5).astype(jnp.float32)


def relax(source, rigidity_field):
    diagonal = MASS_TERM + jnp.zeros_like(rigidity_field)
    face_pairs = []
    for dim_index in (1, 2, 3):
        dim_size = rigidity_field.shape[dim_index]
        forward_nb = jnp.concatenate([lax.slice_in_dim(rigidity_field, 1, dim_size, axis=dim_index), lax.slice_in_dim(rigidity_field, dim_size - 1, dim_size, axis=dim_index)], dim_index)
        backward_nb = jnp.concatenate([lax.slice_in_dim(rigidity_field, 0, 1, axis=dim_index), lax.slice_in_dim(rigidity_field, 0, dim_size - 1, axis=dim_index)], dim_index)
        forward = 0.5 * (rigidity_field + forward_nb)
        backward = 0.5 * (rigidity_field + backward_nb)
        diagonal = diagonal + forward + backward
        face_pairs.append((dim_index + 1, forward[:, None], backward[:, None]))
    step_scale = RELAX_WEIGHT / diagonal[:, None]
    iterate = step_scale * source
    for sweep_index in range(SWEEPS - 1):
        applied = diagonal[:, None] * iterate
        for field_dim, forward, backward in face_pairs:
            dim_size = iterate.shape[field_dim]
            zero_slab = jnp.zeros_like(lax.slice_in_dim(iterate, 0, 1, axis=field_dim))
            next_vals = jnp.concatenate([lax.slice_in_dim(iterate, 1, dim_size, axis=field_dim), zero_slab], field_dim)
            prev_vals = jnp.concatenate([zero_slab, lax.slice_in_dim(iterate, 0, dim_size - 1, axis=field_dim)], field_dim)
            applied = applied - forward * next_vals - backward * prev_vals
        iterate = iterate + step_scale * (source - applied)
    return iterate


def intersection_add(windows, axis, stride):
    window_count = windows.shape[0]
    length = windows.shape[axis + 1]
    extra_len = length - stride
    leading = lax.slice_in_dim(windows, 0, stride, axis=axis + 1)
    trailing = lax.slice_in_dim(windows, stride, length, axis=axis + 1)
    padding = [(0, 0)] * windows.ndim
    padding[axis + 1] = (0, stride - extra_len)
    trailing = jnp.pad(trailing, padding)

    def flatten(blocks):
        shifted = jnp.moveaxis(blocks, 0, axis)
        new_shape = list(blocks.shape[1:])
        new_shape[axis] = window_count * stride
        return shifted.reshape(new_shape)

    main_part = flatten(leading)
    tail_part = flatten(trailing)
    pad_main = [(0, 0)] * main_part.ndim
    pad_main[axis] = (0, extra_len)
    pad_tail = [(0, 0)] * main_part.ndim
    pad_tail[axis] = (stride, 0)
    tail_full = lax.slice_in_dim(jnp.pad(tail_part, pad_tail), 0, window_count * stride + extra_len, axis=axis)
    return jnp.pad(main_part, pad_main) + tail_full


def reference(equation_misfit, thermal_excess, spanning_vectors, global_solve_pieces, influencing_partition_table, spanning_vector_tally):
    rigidity_field = rigidity_magnitude(thermal_excess)
    stacked = jnp.concatenate([equation_misfit, rigidity_field[None]], 0)
    padded = jnp.pad(stacked, ((0, 0), (0, 0), (OV, OV), (OV, OV)))
    weight_rows = unity_weights(SX + 2 * OV)
    weight_cols = unity_weights(CY + 2 * OV)
    residual_low = equation_misfit.astype(jnp.bfloat16)
    kept = jnp.arange(KMAX)[None, None, :] < spanning_vector_tally[:, :, None]

    def restrict(strip_index):
        begin_row = (strip_index * SX).astype(jnp.int32)
        strip_res = lax.dynamic_slice_in_dim(residual_low, begin_row, SX, 2).astype(jnp.float32).reshape(3, VERTICAL_LAYERS, SX, SUBY, CY)
        strip_vec = lax.dynamic_slice_in_dim(spanning_vectors, begin_row, SX, 3).astype(jnp.float32).reshape(KMAX, 3, VERTICAL_LAYERS, SX, SUBY, CY)
        return jnp.einsum('kcdxjy,cdxjy->jk', strip_vec, strip_res, precision=lax.Precision.HIGHEST)

    coarse_rhs = lax.map(restrict, jnp.arange(SUBX))
    coarse_rhs = jnp.where(kept, coarse_rhs, 0.0)
    flat_rhs = coarse_rhs.reshape(SUBX * SUBY, KMAX)
    fetched = flat_rhs[influencing_partition_table]
    coarse_sol = jnp.einsum('abljk,ablk->abj', global_solve_pieces, fetched, precision=lax.Precision.HIGHEST)
    coarse_sol = jnp.where(kept, coarse_sol, 0.0)
    coarse_low = coarse_sol.astype(jnp.bfloat16)

    def add_strip(strip_index, accumulator):
        begin_row = (strip_index * SX).astype(jnp.int32)
        strip_block = lax.dynamic_slice_in_dim(padded, begin_row, SX + 2 * OV, 2)

        def cut_window(column_start):
            return lax.dynamic_slice_in_dim(strip_block, column_start, CY + 2 * OV, 3)

        windows = jax.vmap(cut_window)((jnp.arange(SUBY) * CY).astype(jnp.int32))
        corrected = relax(windows[:, :3], windows[:, 3])
        corrected = corrected * weight_rows[:, None] * weight_cols
        strip_sum = intersection_add(corrected, 3, CY)
        current = lax.dynamic_slice_in_dim(accumulator, begin_row, SX + 2 * OV, 2)
        return lax.dynamic_update_slice_in_dim(accumulator, current + strip_sum, begin_row, 2)

    accumulator = jnp.zeros((3, VERTICAL_LAYERS, MESH_NORTHWARD + 2 * OV, MESH_EASTWARD + 2 * OV), jnp.float32)
    accumulator = lax.fori_loop(0, SUBX, add_strip, accumulator)
    local_part = accumulator[:, :, OV:OV + MESH_NORTHWARD, OV:OV + MESH_EASTWARD]

    def prolong(strip_index):
        begin_row = (strip_index * SX).astype(jnp.int32)
        strip_vec = lax.dynamic_slice_in_dim(spanning_vectors, begin_row, SX, 3).astype(jnp.float32).reshape(KMAX, 3, VERTICAL_LAYERS, SX, SUBY, CY)
        strip_sol = lax.dynamic_index_in_dim(coarse_low, strip_index, 0, keepdims=False).astype(jnp.float32)
        return jnp.einsum('kcdxjy,jk->cdxjy', strip_vec, strip_sol, precision=lax.Precision.HIGHEST).reshape(3, VERTICAL_LAYERS, SX, MESH_EASTWARD)

    prolonged = lax.map(prolong, jnp.arange(SUBX))
    prolonged = jnp.moveaxis(prolonged, 0, 2).reshape(3, VERTICAL_LAYERS, MESH_NORTHWARD, MESH_EASTWARD)
    return local_part + prolonged
```

```python
import jax
import jax.numpy as jnp
from jax import lax
from jax.experimental import pallas as pl
from jax.experimental.pallas import tpu as pltpu
from jax.sharding import PartitionSpec as P

F32 = jnp.float32
BF16 = jnp.bfloat16
MESH = pl.DeviceIdType.MESH

COMPS = 3
DEPTH = 16
ROWS = 64
LANES = 128
SUBS = 4
SX = 16
KMAX = 8
NLIST = 9

MASS_TERM = 0.05
RELAX_WEIGHT = 0.8
ARRHENIUS_FACTOR = 6.0


def kernel(
    b_hbm,
    te_hbm,
    v_hbm,
    g_ref,
    table_ref,
    tally_ref,
    out_hbm,
    te_t,
    b_t,
    b_n,
    v_n,
    shear,
    shear_lr,
    edge_own,
    edge_got,
    rows_own,
    rows_got,
    corner_got,
    edge_m,
    edge_x,
    shift,
    x0,
    x1,
    lhs0,
    lhs1,
    lr0,
    lr1,
    s0,
    s1,
    gl,
    gr,
    xr0,
    xr1,
    lhsr0,
    lhsr1,
    lrr0,
    lrr1,
    sr0,
    sr1,
    loc_t,
    loc_n,
    gx_pieces,
    coarse,
    sol,
    te_sem,
    bt_sem,
    bn_sem,
    v_sem,
    loc_sem,
    out_sem,
    halo_send,
    halo_recv,
    one_send,
    one_recv,
    two_send,
    two_recv,
):
    gx = lax.axis_index("gx")
    gy = lax.axis_index("gy")
    nx = lax.axis_size("gx")
    ny = lax.axis_size("gy")
    up, down = lax.rem(gx + nx - 1, nx), lax.rem(gx + 1, nx)
    left, right = lax.rem(gy + ny - 1, ny), lax.rem(gy + 1, ny)

    barrier = pltpu.get_barrier_semaphore()
    for o in range(1, nx):
        pl.semaphore_signal(barrier, 1, device_id=(lax.rem(gx + o, nx), gy), device_id_type=MESH)
    for o in range(1, ny):
        pl.semaphore_signal(barrier, 1, device_id=(gx, lax.rem(gy + o, ny)), device_id_type=MESH)
    for px in (up, down):
        for py in (left, right):
            pl.semaphore_signal(barrier, 1, device_id=(px, py), device_id_type=MESH)

    for d in range(DEPTH):
        pltpu.make_async_copy(te_hbm.at[d], te_t.at[:, d, :], te_sem).start()
    for c in range(COMPS):
        for d in range(DEPTH):
            pltpu.make_async_copy(b_hbm.at[c, d], b_t.at[c, :, d, :], bt_sem).start()
    pltpu.make_async_copy(b_hbm, b_n, bn_sem).start()
    half = DEPTH // 2

    def v_copy(c, h):
        part = pl.ds(h * half, half)
        return pltpu.make_async_copy(
            v_hbm.at[:, c, part], v_n.at[:, c, part], v_sem.at[c * 2 + h]
        )

    for c in range(COMPS):
        for h in range(2):
            v_copy(c, h).start()

    lane = lax.broadcasted_iota(jnp.int32, (DEPTH, LANES), 1)
    sub = lax.broadcasted_iota(jnp.int32, (DEPTH, LANES), 0)

    wi = lax.broadcasted_iota(jnp.int32, (2 * LANES, 2 * LANES), 0)
    wj = lax.broadcasted_iota(jnp.int32, (2 * LANES, 2 * LANES), 1)
    own, to_left = wi < LANES, wj < LANES
    hit = (
        (own & to_left & (wi == wj - 1))
        | (own & ~to_left & (wi == wj - LANES + 1))
        | (~own & ((wi & 3) == 3) & (wj == 0))
        | (~own & ((wi & 3) == 0) & (wj == 2 * LANES - 1))
    )
    shift[...] = jnp.where(hit, 1.0, 0.0).astype(BF16)

    ei = lax.broadcasted_iota(jnp.int32, (KMAX, LANES), 0)
    ej = lax.broadcasted_iota(jnp.int32, (KMAX, LANES), 1)
    spread = jnp.where(((ej & (KMAX - 1)) == ei) & (ej < SUBS * KMAX), 1.0, 0.0)
    gx_pieces[...] = jnp.dot(
        g_ref[...].reshape(SUBS * NLIST * KMAX, KMAX),
        spread,
        precision=lax.Precision.HIGHEST,
        preferred_element_type=F32,
    )

    zeros = jnp.zeros((COMPS, 8, LANES), F32)

    def clear(p, _):
        for ref in (x0, x1):
            ref[:, p, 0:8, :] = zeros
            ref[:, p, 24:32, :] = zeros
        return 0

    lax.fori_loop(0, ROWS + 2, clear, 0)

    def clear_cut(p, _):
        for ref in (xr0, xr1):
            ref[:, p, 0:8, :] = zeros
            ref[:, p, 24:32, :] = zeros
        return 0

    lax.fori_loop(0, 2 * SUBS, clear_cut, 0)

    def put_shear(p, m):
        shear[p, 8:24, :] = m
        shear[p, 7:8, :] = m[0:1]
        shear[p, 24:25, :] = m[15:16]

    pltpu.make_async_copy(te_t, te_t, te_sem).wait()

    def make_shear(i, _):
        for j in range(4):
            r = i * 4 + j
            m = 1.0 / (1.0 + jnp.exp(ARRHENIUS_FACTOR * (1.0 - 1.0 / te_t[r])))
            put_shear(r + 2, m)
        return 0

    lax.fori_loop(0, ROWS // 4, make_shear, 0)
    pltpu.make_async_copy(b_t, b_t, bt_sem).wait()

    slot = ((lane + 2) & (LANES - 1)) >> 2

    def pack(i, held):
        for j in range(2):
            rr = i * 2 + j
            here = slot == rr
            new = []
            for f in range(4):
                for h in range(2):
                    r = rr + 32 * h
                    val = shear[r + 2, 8:24, :] if f == 0 else b_t[f - 1, r]
                    new.append(jnp.where(here, pltpu.roll(val, 4 * rr, 1), held[f * 2 + h]))
            held = tuple(new)
        return held

    packed = lax.fori_loop(0, 16, pack, tuple(jnp.zeros((DEPTH, LANES), F32) for _ in range(8)))
    for i in range(8):
        edge_own[i] = packed[i]
    for side, (near, next_) in enumerate(((0, 1), (ROWS - 1, ROWS - 2))):
        rows_own[side, 0] = shear[near + 2, 8:24, :]
        rows_own[side, 1] = shear[next_ + 2, 8:24, :]
        for c in range(COMPS):
            rows_own[side, 2 + c] = b_t[c, near]

    pl.semaphore_wait(barrier, (nx - 1) + (ny - 1) + 4)

    def halo(i, src, dst, px, py):
        return pltpu.make_async_remote_copy(
            src_ref=src,
            dst_ref=dst,
            send_sem=halo_send.at[i],
            recv_sem=halo_recv.at[i],
            device_id=(px, py),
            device_id_type=MESH,
        )

    halos = [
        halo(0, rows_own.at[0], rows_got.at[1], up, gy),
        halo(1, rows_own.at[1], rows_got.at[0], down, gy),
        halo(2, edge_own, edge_got.at[1], gx, left),
        halo(3, edge_own, edge_got.at[0], gx, right),
        halo(4, rows_own.at[0, 0], corner_got.at[3], up, left),
        halo(5, rows_own.at[0, 0], corner_got.at[2], up, right),
        halo(6, rows_own.at[1, 0], corner_got.at[1], down, left),
        halo(7, rows_own.at[1, 0], corner_got.at[0], down, right),
    ]
    for copy in halos:
        copy.start()

    pltpu.make_async_copy(b_n, b_n, bn_sem).wait()
    accs = tuple(jnp.zeros((8, LANES), F32) for _ in range(SUBS * KMAX))
    for c in range(COMPS):
        for h in range(2):
            v_copy(c, h).wait()

            def restrict(d, accs):
                new = []
                for s in range(SUBS):
                    part = slice(s * SX, s * SX + SX)
                    low = b_n[c, d, part, :].astype(BF16).astype(F32)
                    for k in range(KMAX):
                        prod = v_n[k, c, d, part, :].astype(F32) * low
                        new.append(accs[s * KMAX + k] + (prod[:8] + prod[8:]))
                return tuple(new)

            accs = lax.fori_loop(h * half, h * half + half, restrict, accs)
    sums = jnp.stack(accs).sum(axis=1)
    totals = jnp.sum(sums, axis=1, keepdims=True)
    ri = lax.broadcasted_iota(jnp.int32, (SUBS * KMAX, LANES), 0)
    rj = lax.broadcasted_iota(jnp.int32, (SUBS * KMAX, LANES), 1)
    rhs = jnp.sum(jnp.where(ri == rj, totals, 0.0), axis=0, keepdims=True)
    lane1 = lax.broadcasted_iota(jnp.int32, (1, LANES), 1)
    limit = jnp.zeros((1, LANES), jnp.int32)
    for s in range(SUBS):
        limit = jnp.where((lane1 >> 3) == s, tally_ref[s, 0], limit)
    rhs = jnp.where((lane1 & (KMAX - 1)) < limit, rhs, 0.0)
    coarse[gy * nx + gx] = rhs

    def one(o, who):
        slot_ref = coarse.at[gy * nx + who]
        return pltpu.make_async_remote_copy(
            src_ref=slot_ref,
            dst_ref=slot_ref,
            send_sem=one_send.at[o - 1],
            recv_sem=one_recv.at[o - 1],
            device_id=(lax.rem(gx + o, nx), gy),
            device_id_type=MESH,
        )

    def two(o, who):
        slot_ref = coarse.at[pl.ds(who * nx, nx)]
        return pltpu.make_async_remote_copy(
            src_ref=slot_ref,
            dst_ref=slot_ref,
            send_sem=two_send.at[o - 1],
            recv_sem=two_recv.at[o - 1],
            device_id=(gx, lax.rem(gy + o, ny)),
            device_id_type=MESH,
        )

    for o in range(1, nx):
        one(o, gx).start()

    for copy in halos:
        copy.wait()

    def flag(cond):
        return jnp.where(cond, 1.0, 0.0).astype(F32)

    k_up, k_down = flag(gx > 0), flag(gx < nx - 1)
    k_left, k_right = flag(gy > 0), flag(gy < ny - 1)
    put_shear(1, rows_got[0, 0] * k_up)
    put_shear(0, rows_got[0, 1] * k_up)
    put_shear(ROWS + 2, rows_got[1, 0] * k_down)
    put_shear(ROWS + 3, rows_got[1, 1] * k_down)
    from_left = (lane & 3) >= 2
    got = [
        jnp.where(from_left, edge_got[0, i] * k_left, edge_got[1, i] * k_right) for i in range(8)
    ]
    corner_up = jnp.where(lane == LANES - 1, corner_got[0] * (k_up * k_left), corner_got[1] * (k_up * k_right))
    corner_down = jnp.where(lane == LANES - 1, corner_got[2] * (k_down * k_left), corner_got[3] * (k_down * k_right))
    first, last = slot == 0, slot == 31
    back4 = LANES - 4
    ups = [
        jnp.where(first, corner_up, pltpu.roll(got[0], 4, 1)),
        jnp.where(first, pltpu.roll(got[0], 4, 1), pltpu.roll(got[1], 4, 1)),
    ]
    downs = [
        jnp.where(last, pltpu.roll(got[1], back4, 1), pltpu.roll(got[0], back4, 1)),
        jnp.where(last, pltpu.roll(corner_down, back4, 1), pltpu.roll(got[1], back4, 1)),
    ]
    spot = slot & (SX - 1)
    for h in range(2):
        m, mine = got[h], packed[h]
        sides = jnp.where(
            (lane & 3) == 3,
            pltpu.roll(m, 1, 1) + pltpu.roll(mine, LANES - 1, 1),
            pltpu.roll(m, LANES - 1, 1) + pltpu.roll(mine, 1, 1),
        )
        over = jnp.where(sub == 0, m, pltpu.roll(m, 1, 0))
        under = jnp.where(sub == DEPTH - 1, m, pltpu.roll(m, DEPTH - 1, 0))
        diag = MASS_TERM + 3.0 * m + 0.5 * (ups[h] + downs[h] + sides + over + under)
        cut = jnp.where(spot == 7, m - downs[h], jnp.where(spot == 8, m - ups[h], 0.0))
        scale = RELAX_WEIGHT / diag
        scale_cut = RELAX_WEIGHT / (diag + 0.5 * cut)
        edge_m[h] = m
        for c in range(COMPS):
            edge_x[0, h, c] = scale * got[2 + 2 * c + h]
            edge_x[1, h, c] = scale_cut * got[2 + 2 * c + h]

    lane3 = lax.broadcasted_iota(jnp.int32, (SX, DEPTH, LANES), 2)
    plane3 = lax.broadcasted_iota(jnp.int32, (SX, DEPTH, LANES), 0)
    pair3 = ((lane3 + 1) & (LANES - 1)) >> 1
    pair = ((lane + 1) & (LANES - 1)) >> 1

    def shear_sides(s, _):
        base = s * SX
        mine = shear[pl.ds(base + 2, SX), 8:24, :]
        theirs = jnp.where(pair3 == 2 * ((plane3 + base) & 31), edge_m[s // 2][None], 0.0)
        both = jnp.concatenate([mine, theirs], axis=2).astype(BF16)
        moved = jnp.dot(both.reshape(SX * DEPTH, 2 * LANES), shift[...], preferred_element_type=F32)
        shear_lr[pl.ds(base + 1, SX)] = moved.reshape(SX, DEPTH, 2 * LANES)
        return 0

    lax.fori_loop(0, SUBS, shear_sides, 0)
    ends = jnp.concatenate(
        [
            jnp.concatenate([shear[1, 8:24, :], jnp.where(pair == 0, corner_up, 0.0)], axis=1),
            jnp.concatenate([shear[ROWS + 2, 8:24, :], jnp.where(pair == 0, corner_down, 0.0)], axis=1),
        ],
        axis=0,
    ).astype(BF16)
    moved = jnp.dot(ends, shift[...], preferred_element_type=F32)
    shear_lr[0] = moved[:DEPTH]
    shear_lr[ROWS + 1] = moved[DEPTH:]

    def first_sweep(p):
        m = shear[p + 1, 8:24, :]
        mu, md = shear[p, 8:24, :], shear[p + 2, 8:24, :]
        mo, mb = shear[p + 1, 7:23, :], shear[p + 1, 9:25, :]
        ml, mr = shear_lr[p, :, :LANES], shear_lr[p, :, LANES:]
        diag = MASS_TERM + 3.0 * m + 0.5 * ((mu + md) + (ml + mr) + (mo + mb))
        cut = 0.5 * jnp.where(lane == 7, m - mr, jnp.where(lane == 120, m - ml, 0.0))
        return m, mu, md, ml, mr, diag, cut

    for p, side, keep in ((0, 0, k_up), (ROWS + 1, 1, k_down)):
        _, _, _, _, _, diag, cut = first_sweep(p)
        b = rows_got[side, 2:5] * keep
        x0[:, p, 8:24, :] = (RELAX_WEIGHT / diag) * b
        x1[:, p, 8:24, :] = (RELAX_WEIGHT / (diag + cut)) * b

    def sweep_block(s, _):
        for q in range(SX):
            r = s * SX + q
            m, mu, md, ml, mr, diag, cut = first_sweep(r + 1)
            b = b_t[:, r]
            here = pair == 2 * (r & 31)
            gl[r] = m + ml
            gr[r] = m + mr
            theirs = jnp.where(here, edge_x[0, s // 2], 0.0).astype(BF16)
            for store, dg, xs, ls in ((s0, diag, x0, lhs0), (s1, diag + cut, x1, lhs1)):
                scale = RELAX_WEIGHT / dg
                store[r] = scale
                x = scale * b
                xs[:, r + 1, 8:24, :] = x
                ls[r, :, :, :LANES] = x.astype(BF16)
                ls[r, :, :, LANES:] = theirs
            if q in (7, 8):
                e = s * 2 + (q - 7)
                diag = diag + 0.5 * (m - (md if q == 7 else mu))
                theirs = jnp.where(here, edge_x[1, s // 2], 0.0).astype(BF16)
                for store, dg, xs, ls in ((sr0, diag, xr0, lhsr0), (sr1, diag + cut, xr1, lhsr1)):
                    scale = RELAX_WEIGHT / dg
                    store[e] = scale
                    x = scale * b
                    xs[:, e, 8:24, :] = x
                    ls[e, :, :, :LANES] = x.astype(BF16)
                    ls[e, :, :, LANES:] = theirs
        return 0

    lax.fori_loop(0, SUBS, sweep_block, 0)

    for o in range(1, nx):
        one(o, gx).wait_send()
        one(o, lax.rem(gx + nx - o, nx)).wait_recv()
    for o in range(1, ny):
        two(o, gy).start()

    block = 8

    def sides(i, _):
        for ls, ds in ((lhs0, lr0), (lhs1, lr1)):
            rows = ls[pl.ds(i * block, block)].reshape(block * COMPS * DEPTH, 2 * LANES)
            moved = jnp.dot(rows, shift[...], preferred_element_type=F32)
            ds[pl.ds(i * block, block)] = moved.reshape(block, COMPS, DEPTH, 2 * LANES)
        return 0

    lax.fori_loop(0, ROWS // block, sides, 0)
    for ls, ds in ((lhsr0, lrr0), (lhsr1, lrr1)):
        rows = ls[...].reshape(2 * SUBS * COMPS * DEPTH, 2 * LANES)
        moved = jnp.dot(rows, shift[...], preferred_element_type=F32)
        ds[...] = moved.reshape(2 * SUBS, COMPS, DEPTH, 2 * LANES)

    edge_lo, edge_hi = lane < 8, lane >= 120
    w0 = jnp.where(edge_lo | edge_hi, 0.25, 0.5).astype(F32)
    w1 = jnp.where(edge_lo, 0.25 * k_left, jnp.where(edge_hi, 0.25 * k_right, 0.0)).astype(F32)

    def second_block(s, _):
        for q in range(SX):
            r = s * SX + q
            m = shear[r + 2, 8:24, :]
            gu, gd = m + shear[r + 1, 8:24, :], m + shear[r + 3, 8:24, :]
            go, gb = m + shear[r + 2, 7:23, :], m + shear[r + 2, 9:25, :]
            g_l, g_r = gl[r], gr[r]
            if q < 8:
                keep = jnp.where((gx == 0) & (s == 0), 0.5, 1.0)
            else:
                keep = jnp.where((gx == nx - 1) & (s == SUBS - 1), 0.5, 1.0)
            b24 = b_t[:, r] * 2.4
            results = []
            for v, (ss, xs, lr, ssr, xsr, lrr) in enumerate(
                ((s0, x0, lr0, sr0, xr0, lrr0), (s1, x1, lr1, sr1, xr1, lrr1))
            ):
                hl = g_l if v == 0 else jnp.where(lane == 120, 0.0, g_l)
                hr = g_r if v == 0 else jnp.where(lane == 7, 0.0, g_r)
                scale = ss[r]
                above, below = xs[:, r, 8:24, :], xs[:, r + 2, 8:24, :]
                total = (b24 + gu * above + gd * below) + (
                    go * xs[:, r + 1, 7:23, :] + gb * xs[:, r + 1, 9:25, :]
                )
                total = total + (hl * lr[r, :, :, :LANES] + hr * lr[r, :, :, LANES:])
                x = scale * total
                if q in (6, 7, 8, 9):
                    e = s * 2 + (0 if q < 8 else 1)
                    if q == 6:
                        y = x + (scale * gd) * (xsr[:, e, 8:24, :] - below)
                    elif q == 9:
                        y = x + (scale * gu) * (xsr[:, e, 8:24, :] - above)
                    else:
                        other = gu * above if q == 7 else gd * below
                        y = (b24 + other) + (go * xsr[:, e, 7:23, :] + gb * xsr[:, e, 9:25, :])
                        y = y + (hl * lrr[e, :, :, :LANES] + hr * lrr[e, :, :, LANES:])
                        y = ssr[e] * y
                    x = 0.5 * x + (keep - 0.5) * y
                results.append(x)
            z0, z1 = results
            if q in (6, 7, 8, 9):
                loc_t[:, r] = w0 * z0 + w1 * z1
            else:
                loc_t[:, r] = (keep * w0) * z0 + (keep * w1) * z1
        return 0

    lax.fori_loop(0, SUBS, second_block, 0)
    for c in range(COMPS):
        for d in range(DEPTH):
            pltpu.make_async_copy(loc_t.at[c, :, d, :], loc_n.at[c, d], loc_sem).start()

    for o in range(1, ny):
        two(o, gy).wait_send()
        two(o, lax.rem(gy + ny - o, ny)).wait_recv()
    lane8 = lax.broadcasted_iota(jnp.int32, (KMAX, LANES), 1)
    sub8 = lax.broadcasted_iota(jnp.int32, (KMAX, LANES), 0)
    for s in range(SUBS):
        acc = jnp.zeros((KMAX, LANES), F32)
        for l in range(NLIST):
            n = table_ref[s, 0, l]
            row = coarse[(n & (ny - 1)) * nx + (n >> 6)]
            which = (n >> 4) & (SUBS - 1)
            row = jnp.where((lane1 >> 3) == which, row, 0.0)
            base = (s * NLIST + l) * KMAX
            acc = acc + gx_pieces[base : base + KMAX, :] * row
        answer = jnp.broadcast_to(jnp.sum(acc, axis=1, keepdims=True), (KMAX, LANES))
        answer = jnp.where(sub8 < tally_ref[s, 0], answer, 0.0)
        sol[s] = answer.astype(BF16).astype(F32)
    pltpu.make_async_copy(loc_n, loc_n, loc_sem).wait()

    def out_copy(s):
        part = pl.ds(s * SX, SX)
        return pltpu.make_async_copy(loc_n.at[:, :, part], out_hbm.at[:, :, part], out_sem.at[s])

    for s in range(SUBS):
        part = slice(s * SX, s * SX + SX)
        weights = [jnp.broadcast_to(sol[s, k : k + 1, :], (SX, LANES)) for k in range(KMAX)]

        def prolong(i, _):
            for j in range(4):
                d = i * 4 + j
                for c in range(COMPS):
                    total = loc_n[c, d, part, :]
                    for k in range(KMAX):
                        total = total + v_n[k, c, d, part, :].astype(F32) * weights[k]
                    loc_n[c, d, part, :] = total
            return 0

        lax.fori_loop(0, DEPTH // 4, prolong, 0)
        out_copy(s).start()
    for s in range(SUBS):
        out_copy(s).wait()


def local(
    equation_misfit,
    thermal_excess,
    spanning_vectors,
    global_solve_pieces,
    influencing_partition_table,
    spanning_vector_tally,
):
    nx, ny = lax.axis_size("gx"), lax.axis_size("gy")
    hbm = pl.BlockSpec(memory_space=pltpu.HBM)
    smem = pl.BlockSpec(memory_space=pltpu.SMEM)
    vmem = pl.BlockSpec(memory_space=pltpu.VMEM)
    plane = (DEPTH, LANES)
    wide = (DEPTH, 2 * LANES)
    cuts = 2 * SUBS

    def f32(*shape):
        return pltpu.VMEM(shape, F32)

    def low(*shape):
        return pltpu.VMEM(shape, BF16)

    dma = pltpu.SemaphoreType.DMA
    scratch = [
        f32(ROWS, *plane),
        f32(COMPS, ROWS, *plane),
        f32(COMPS, DEPTH, ROWS, LANES),
        low(KMAX, COMPS, DEPTH, ROWS, LANES),
        f32(ROWS + 4, 32, LANES),
        f32(ROWS + 2, *wide),
        f32(8, *plane),
        f32(2, 8, *plane),
        f32(2, 5, *plane),
        f32(2, 5, *plane),
        f32(4, *plane),
        f32(2, *plane),
        f32(2, 2, COMPS, *plane),
        low(2 * LANES, 2 * LANES),
        f32(COMPS, ROWS + 2, 32, LANES),
        f32(COMPS, ROWS + 2, 32, LANES),
        low(ROWS, COMPS, *wide),
        low(ROWS, COMPS, *wide),
        f32(ROWS, COMPS, *wide),
        f32(ROWS, COMPS, *wide),
        f32(ROWS, *plane),
        f32(ROWS, *plane),
        f32(ROWS, *plane),
        f32(ROWS, *plane),
        f32(COMPS, cuts, 32, LANES),
        f32(COMPS, cuts, 32, LANES),
        low(cuts, COMPS, *wide),
        low(cuts, COMPS, *wide),
        f32(cuts, COMPS, *wide),
        f32(cuts, COMPS, *wide),
        f32(cuts, *plane),
        f32(cuts, *plane),
        f32(COMPS, ROWS, *plane),
        f32(COMPS, DEPTH, ROWS, LANES),
        f32(SUBS * NLIST * KMAX, LANES),
        f32(nx * ny, 1, LANES),
        f32(SUBS, KMAX, LANES),
        dma,
        dma,
        dma,
        dma((2 * COMPS,)),
        dma,
        dma((SUBS,)),
        dma((8,)),
        dma((8,)),
        dma((nx - 1,)),
        dma((nx - 1,)),
        dma((ny - 1,)),
        dma((ny - 1,)),
    ]
    return pl.pallas_call(
        kernel,
        out_shape=jax.ShapeDtypeStruct(equation_misfit.shape, F32),
        in_specs=[hbm, hbm, hbm, vmem, smem, smem],
        out_specs=hbm,
        scratch_shapes=scratch,
        compiler_params=pltpu.CompilerParams(
            collective_id=0, has_side_effects=True, vmem_limit_bytes=56 * 2**20
        ),
        name="schwarz",
    )(
        equation_misfit,
        thermal_excess,
        spanning_vectors,
        global_solve_pieces,
        influencing_partition_table,
        spanning_vector_tally,
    )


def solution(mesh):
    return jax.shard_map(
        local,
        mesh=mesh,
        in_specs=(
            P(None, None, "gx", "gy"),
            P(None, "gx", "gy"),
            P(None, None, None, "gx", "gy"),
            P("gx", "gy", None, None, None),
            P("gx", "gy", None),
            P("gx", "gy"),
        ),
        out_specs=P(None, None, "gx", "gy"),
        check_vma=False,
    )
```

```python
import jax
import jax.numpy as jnp
from jax import lax
from jax.experimental import pallas as pl
from jax.experimental.pallas import tpu as pltpu
from jax.sharding import PartitionSpec as P

F32 = jnp.float32
BF16 = jnp.bfloat16
MESH = pl.DeviceIdType.MESH

COMPS = 3
DEPTH = 16
ROWS = 64
LANES = 128
SUBS = 4
SX = 16
KMAX = 8
NLIST = 9

MASS_TERM = 0.05
RELAX_WEIGHT = 0.8
ARRHENIUS_FACTOR = 6.0


def kernel(
    b_hbm,
    te_hbm,
    v_hbm,
    g_hbm,
    table_ref,
    tally_ref,
    loc_n,
    v_n,
    sol,
    te_t,
    b_t,
    b_n,
    pieces,
    shear,
    shear_lr,
    edge_own,
    edge_got,
    rows_own,
    rows_got,
    corner_got,
    edge_m,
    edge_x,
    edge_q,
    shift,
    x0,
    lhs,
    moved,
    s0,
    s1,
    q1,
    gl,
    gr,
    sr,
    qr,
    qr_lr,
    loc_t,
    sums,
    parts,
    coarse,
    te_sem,
    bt_sem,
    bn_sem,
    g_sem,
    v_sem,
    loc_sem,
    halo_send,
    halo_recv,
    one_send,
    one_recv,
    two_send,
    two_recv,
):
    gx = lax.axis_index("gx")
    gy = lax.axis_index("gy")
    nx = lax.axis_size("gx")
    ny = lax.axis_size("gy")
    up, down = lax.rem(gx + nx - 1, nx), lax.rem(gx + 1, nx)
    left, right = lax.rem(gy + ny - 1, ny), lax.rem(gy + 1, ny)

    for d in range(DEPTH):
        pltpu.make_async_copy(te_hbm.at[d], te_t.at[:, d, :], te_sem).start()
    for d in range(DEPTH):
        pltpu.make_async_copy(b_hbm.at[:, d], b_t.at[:, :, d, :], bt_sem).start()
    pltpu.make_async_copy(b_hbm, b_n, bn_sem).start()
    half = DEPTH // 2

    def v_copy(i):
        part = pl.ds((i % 2) * half, half)
        return pltpu.make_async_copy(
            v_hbm.at[:, i // 2, part], v_n.at[:, i // 2, part], v_sem.at[i]
        )

    for i in range(2 * COMPS):
        v_copy(i).start()
    for a in range(KMAX):
        pltpu.make_async_copy(g_hbm.at[:, 0, a], pieces.at[:, :, a, :], g_sem).start()

    barrier = pltpu.get_barrier_semaphore()
    for o in range(1, nx):
        pl.semaphore_signal(barrier, 1, device_id=(lax.rem(gx + o, nx), gy), device_id_type=MESH)
    for o in range(1, ny):
        pl.semaphore_signal(barrier, 1, device_id=(gx, lax.rem(gy + o, ny)), device_id_type=MESH)
    for px in (up, down):
        for py in (left, right):
            pl.semaphore_signal(barrier, 1, device_id=(px, py), device_id_type=MESH)

    lane = lax.broadcasted_iota(jnp.int32, (DEPTH, LANES), 1)
    sub = lax.broadcasted_iota(jnp.int32, (DEPTH, LANES), 0)

    wi = lax.broadcasted_iota(jnp.int32, (2 * LANES, 2 * LANES), 0)
    wj = lax.broadcasted_iota(jnp.int32, (2 * LANES, 2 * LANES), 1)
    own, to_left = wi < LANES, wj < LANES
    hit = (
        (own & to_left & (wi == wj - 1))
        | (own & ~to_left & (wi == wj - LANES + 1))
        | (~own & ((wi & 3) == 3) & (wj == 0))
        | (~own & ((wi & 3) == 0) & (wj == 2 * LANES - 1))
    )
    shift[...] = jnp.where(hit, 1.0, 0.0).astype(BF16)

    zeros = jnp.zeros((COMPS, 8, LANES), F32)
    zero = jnp.zeros((8, LANES), F32)

    def clear(p, _):
        x0[:, p, 0:8, :] = zeros
        x0[:, p, 24:32, :] = zeros
        q1[p, 0:8, :] = zero
        q1[p, 24:32, :] = zero
        return 0

    lax.fori_loop(0, ROWS + 2, clear, 0)

    def clear_cut(p, _):
        for v in range(2):
            qr[v, p, 0:8, :] = zero
            qr[v, p, 24:32, :] = zero
        return 0

    lax.fori_loop(0, 2 * SUBS, clear_cut, 0)
    sums[...] = jnp.zeros(sums.shape, F32)

    def put_shear(p, m):
        shear[p, 8:24, :] = m
        shear[p, 7:8, :] = m[0:1]
        shear[p, 24:25, :] = m[15:16]

    pltpu.make_async_copy(te_t, te_t, te_sem).wait()

    def make_shear(i, _):
        for j in range(4):
            r = i * 4 + j
            m = 1.0 / (1.0 + jnp.exp(ARRHENIUS_FACTOR * (1.0 - 1.0 / te_t[r])))
            put_shear(r + 2, m)
        return 0

    lax.fori_loop(0, ROWS // 4, make_shear, 0)
    pltpu.make_async_copy(b_t, b_t, bt_sem).wait()

    slot = ((lane + 2) & (LANES - 1)) >> 2

    def pack(i, held):
        for j in range(4):
            rr = i * 4 + j
            here = slot == rr
            new = []
            for f in range(4):
                for h in range(2):
                    r = rr + 32 * h
                    val = shear[r + 2, 8:24, :] if f == 0 else b_t[f - 1, r]
                    new.append(jnp.where(here, pltpu.roll(val, 4 * rr, 1), held[f * 2 + h]))
            held = tuple(new)
        return held

    packed = lax.fori_loop(0, 8, pack, tuple(jnp.zeros((DEPTH, LANES), F32) for _ in range(8)))
    for i in range(8):
        edge_own[i] = packed[i]
    for side, (near, next_) in enumerate(((0, 1), (ROWS - 1, ROWS - 2))):
        rows_own[side, 0] = shear[near + 2, 8:24, :]
        rows_own[side, 1] = shear[next_ + 2, 8:24, :]
        for c in range(COMPS):
            rows_own[side, 2 + c] = b_t[c, near]

    pl.semaphore_wait(barrier, (nx - 1) + (ny - 1) + 4)

    def halo(i, src, dst, px, py):
        return pltpu.make_async_remote_copy(
            src_ref=src,
            dst_ref=dst,
            send_sem=halo_send.at[i],
            recv_sem=halo_recv.at[i],
            device_id=(px, py),
            device_id_type=MESH,
        )

    halos = [
        halo(0, rows_own.at[0], rows_got.at[1], up, gy),
        halo(1, rows_own.at[1], rows_got.at[0], down, gy),
        halo(2, edge_own, edge_got.at[1], gx, left),
        halo(3, edge_own, edge_got.at[0], gx, right),
        halo(4, rows_own.at[0, 0], corner_got.at[3], up, left),
        halo(5, rows_own.at[0, 0], corner_got.at[2], up, right),
        halo(6, rows_own.at[1, 0], corner_got.at[1], down, left),
        halo(7, rows_own.at[1, 0], corner_got.at[0], down, right),
    ]
    for copy in halos:
        copy.start()

    pltpu.make_async_copy(b_n, b_n, bn_sem).wait()
    for i in range(2 * COMPS):
        v_copy(i).wait()

        def restrict(s, _):
            part = pl.ds(pl.multiple_of(s * SX, SX), SX)
            c = i // 2
            accs = [sums[s, k] for k in range(KMAX)]
            for j in range(half):
                d = (i % 2) * half + j
                low = b_n[c, d, part, :].astype(BF16).astype(F32)
                for k in range(KMAX):
                    accs[k] = accs[k] + v_n[k, c, d, part, :].astype(F32) * low
            for k in range(KMAX):
                sums[s, k] = accs[k]
            return 0

        lax.fori_loop(0, SUBS, restrict, 0)
    lane8 = lax.broadcasted_iota(jnp.int32, (KMAX, LANES), 1)
    sub8 = lax.broadcasted_iota(jnp.int32, (KMAX, LANES), 0)
    rhs = jnp.zeros((KMAX, LANES), F32)
    for s in range(SUBS):
        total = jnp.sum(jnp.sum(sums[s], axis=1), axis=1, keepdims=True)
        total = jnp.where(sub8 < tally_ref[0, s], total, 0.0)
        rhs = jnp.where(lane8 == gx * SUBS + s, total, rhs)
    parts[gx] = rhs

    def one(o, who):
        return pltpu.make_async_remote_copy(
            src_ref=parts.at[who],
            dst_ref=parts.at[who],
            send_sem=one_send.at[o - 1],
            recv_sem=one_recv.at[o - 1],
            device_id=(lax.rem(gx + o, nx), gy),
            device_id_type=MESH,
        )

    def two(o, who):
        return pltpu.make_async_remote_copy(
            src_ref=coarse.at[who],
            dst_ref=coarse.at[who],
            send_sem=two_send.at[o - 1],
            recv_sem=two_recv.at[o - 1],
            device_id=(gx, lax.rem(gy + o, ny)),
            device_id_type=MESH,
        )

    for o in range(1, nx):
        one(o, gx).start()

    for copy in halos:
        copy.wait()

    def flag(cond):
        return jnp.where(cond, 1.0, 0.0).astype(F32)

    k_up, k_down = flag(gx > 0), flag(gx < nx - 1)
    k_left, k_right = flag(gy > 0), flag(gy < ny - 1)
    put_shear(1, rows_got[0, 0] * k_up)
    put_shear(0, rows_got[0, 1] * k_up)
    put_shear(ROWS + 2, rows_got[1, 0] * k_down)
    put_shear(ROWS + 3, rows_got[1, 1] * k_down)
    from_left = (lane & 3) >= 2
    got = [
        jnp.where(from_left, edge_got[0, i] * k_left, edge_got[1, i] * k_right) for i in range(8)
    ]
    corner_up = jnp.where(
        lane == LANES - 1, corner_got[0] * (k_up * k_left), corner_got[1] * (k_up * k_right)
    )
    corner_down = jnp.where(
        lane == LANES - 1, corner_got[2] * (k_down * k_left), corner_got[3] * (k_down * k_right)
    )
    first, last = slot == 0, slot == 31
    back4 = LANES - 4
    ups = [
        jnp.where(first, corner_up, pltpu.roll(got[0], 4, 1)),
        jnp.where(first, pltpu.roll(got[0], 4, 1), pltpu.roll(got[1], 4, 1)),
    ]
    downs = [
        jnp.where(last, pltpu.roll(got[1], back4, 1), pltpu.roll(got[0], back4, 1)),
        jnp.where(last, pltpu.roll(corner_down, back4, 1), pltpu.roll(got[1], back4, 1)),
    ]
    spot = slot & (SX - 1)
    for h in range(2):
        m, mine = got[h], edge_own[h]
        sides = jnp.where(
            (lane & 3) == 3,
            pltpu.roll(m, 1, 1) + pltpu.roll(mine, LANES - 1, 1),
            pltpu.roll(m, LANES - 1, 1) + pltpu.roll(mine, 1, 1),
        )
        over = jnp.where(sub == 0, m, pltpu.roll(m, 1, 0))
        under = jnp.where(sub == DEPTH - 1, m, pltpu.roll(m, DEPTH - 1, 0))
        diag = MASS_TERM + 3.0 * m + 0.5 * (ups[h] + downs[h] + sides + over + under)
        cut = jnp.where(spot == 7, m - downs[h], jnp.where(spot == 8, m - ups[h], 0.0))
        scale = RELAX_WEIGHT / diag
        edge_m[h] = m
        edge_q[h] = diag / (diag + 0.5 * cut)
        for c in range(COMPS):
            edge_x[h, c] = scale * got[2 + 2 * c + h]

    lane3 = lax.broadcasted_iota(jnp.int32, (SX, DEPTH, LANES), 2)
    plane3 = lax.broadcasted_iota(jnp.int32, (SX, DEPTH, LANES), 0)
    pair3 = ((lane3 + 1) & (LANES - 1)) >> 1
    pair = ((lane + 1) & (LANES - 1)) >> 1

    def shear_sides(s, _):
        base = s * SX
        mine = shear[pl.ds(base + 2, SX), 8:24, :]
        theirs = jnp.where(pair3 == 2 * ((plane3 + base) & 31), edge_m[s // 2][None], 0.0)
        both = jnp.concatenate([mine, theirs], axis=2).astype(BF16)
        result = jnp.dot(both.reshape(SX * DEPTH, 2 * LANES), shift[...], preferred_element_type=F32)
        shear_lr[pl.ds(base + 1, SX)] = result.reshape(SX, DEPTH, 2 * LANES)
        return 0

    lax.fori_loop(0, SUBS, shear_sides, 0)
    ends = jnp.concatenate(
        [
            jnp.concatenate([shear[1, 8:24, :], jnp.where(pair == 0, corner_up, 0.0)], axis=1),
            jnp.concatenate([shear[ROWS + 2, 8:24, :], jnp.where(pair == 0, corner_down, 0.0)], axis=1),
        ],
        axis=0,
    ).astype(BF16)
    result = jnp.dot(ends, shift[...], preferred_element_type=F32)
    shear_lr[0] = result[:DEPTH]
    shear_lr[ROWS + 1] = result[DEPTH:]

    def first_sweep(p):
        m = shear[p + 1, 8:24, :]
        mu, md = shear[p, 8:24, :], shear[p + 2, 8:24, :]
        mo, mb = shear[p + 1, 7:23, :], shear[p + 1, 9:25, :]
        ml, mr = shear_lr[p, :, :LANES], shear_lr[p, :, LANES:]
        diag = MASS_TERM + 3.0 * m + 0.5 * ((mu + md) + (ml + mr) + (mo + mb))
        cut = 0.5 * jnp.where(lane == 7, m - mr, jnp.where(lane == 120, m - ml, 0.0))
        return m, mu, md, ml, mr, diag, cut

    ratio = 1.0 / RELAX_WEIGHT
    for p, side, keep in ((0, 0, k_up), (ROWS + 1, 1, k_down)):
        _, _, _, _, _, diag, cut = first_sweep(p)
        x0[:, p, 8:24, :] = (RELAX_WEIGHT / diag) * (rows_got[side, 2:5] * keep)
        q1[p, 8:24, :] = diag / (diag + cut)

    def sweep_block(s, _):
        for q in range(SX):
            r = s * SX + q
            m, mu, md, ml, mr, diag, cut = first_sweep(r + 1)
            gl[r] = m + ml
            gr[r] = m + mr
            scale = RELAX_WEIGHT / diag
            cut_scale = RELAX_WEIGHT / (diag + cut)
            ratio_diag = ratio * diag
            s0[r] = scale
            s1[r] = cut_scale
            q1[r + 1, 8:24, :] = cut_scale * ratio_diag
            x = scale * b_t[:, r]
            x0[:, r + 1, 8:24, :] = x
            here = pair == 2 * (r & 31)
            lhs[r, :, :, :LANES] = x.astype(BF16)
            lhs[r, :, :, LANES:] = jnp.where(here, edge_x[s // 2], 0.0).astype(BF16)
            if q in (7, 8):
                e = s * 2 + (q - 7)
                diag = diag + 0.5 * (m - (md if q == 7 else mu))
                for v, dg in ((0, diag), (1, diag + cut)):
                    scale = RELAX_WEIGHT / dg
                    sr[v, e] = scale
                    qr[v, e, 8:24, :] = scale * ratio_diag
        return 0

    lax.fori_loop(0, SUBS, sweep_block, 0)
    for v in range(2):
        rows = []
        for e in range(2 * SUBS):
            r = (e // 2) * SX + 7 + e % 2
            theirs = jnp.where(pair == 2 * (r & 31), edge_q[r // 32], 0.0)
            rows.append(jnp.concatenate([qr[v, e, 8:24, :], theirs], axis=1))
        rows = jnp.concatenate(rows, axis=0).astype(BF16)
        result = jnp.dot(rows, shift[...], preferred_element_type=F32)
        qr_lr[v] = result.reshape(2 * SUBS, DEPTH, 2 * LANES)

    edge_lo, edge_hi = lane < 8, lane >= 120
    w0 = jnp.where(edge_lo | edge_hi, 0.25, 0.5).astype(F32)
    w1 = jnp.where(edge_lo, 0.25 * k_left, jnp.where(edge_hi, 0.25 * k_right, 0.0)).astype(F32)
    few = 4

    def second_block(s, _):
        for j in range(SX // few):
            rows = lhs[pl.ds(s * SX + j * few, few)].reshape(few * COMPS * DEPTH, 2 * LANES)
            result = jnp.dot(rows, shift[...], preferred_element_type=F32)
            moved[j * few : (j + 1) * few] = result.reshape(few, COMPS, DEPTH, 2 * LANES)
        for q in range(SX):
            r = s * SX + q
            m = shear[r + 2, 8:24, :]
            gu, gd = m + shear[r + 1, 8:24, :], m + shear[r + 3, 8:24, :]
            go, gb = m + shear[r + 2, 7:23, :], m + shear[r + 2, 9:25, :]
            g_l, g_r = gl[r], gr[r]
            if q < 8:
                keep = jnp.where((gx == 0) & (s == 0), 0.5, 1.0)
            else:
                keep = jnp.where((gx == nx - 1) & (s == SUBS - 1), 0.5, 1.0)
            rest = keep - 0.5
            a0, a1 = w0 * s0[r], w1 * s1[r]
            qu, qd = q1[r, 8:24, :], q1[r + 2, 8:24, :]
            qo, qb = q1[r + 1, 7:23, :], q1[r + 1, 9:25, :]
            qm = q1[r + 1, 8:24, :]
            ql = jnp.where(lane == 121, pltpu.roll(qm, 1, 1), 1.0)
            ql = jnp.where(lane == 120, 0.0, ql)
            qn = jnp.where(lane == 6, pltpu.roll(qm, LANES - 1, 1), 1.0)
            qn = jnp.where(lane == 7, 0.0, qn)
            e = s * 2 + (0 if q < 8 else 1)
            if q in (7, 8):
                r0, r1 = rest * w0 * sr[0, e], rest * w1 * sr[1, e]
                a0, a1 = 0.5 * a0, 0.5 * a1
                ca = a0 + a1 + r0 + r1
                cu = (a0 + r0) + (a1 + r1) * qu if q == 7 else a0 + a1 * qu
                cd = (a0 + r0) + (a1 + r1) * qd if q == 8 else a0 + a1 * qd
                co = (a0 + a1 * qo) + (r0 * qr[0, e, 7:23, :] + r1 * qr[1, e, 7:23, :])
                cb = (a0 + a1 * qb) + (r0 * qr[0, e, 9:25, :] + r1 * qr[1, e, 9:25, :])
                r1l, r1r = jnp.where(lane == 120, 0.0, r1), jnp.where(lane == 7, 0.0, r1)
                cl = (a0 + a1 * ql) + (r0 * qr_lr[0, e, :, :LANES] + r1l * qr_lr[1, e, :, :LANES])
                cr = (a0 + a1 * qn) + (r0 * qr_lr[0, e, :, LANES:] + r1r * qr_lr[1, e, :, LANES:])
            else:
                if q in (6, 9):
                    k0 = 0.5 + rest * qr[0, e, 8:24, :]
                    near = a0 * k0
                    qx = qd if q == 6 else qu
                    near = near + a1 * (0.5 * qx + rest * qr[1, e, 8:24, :])
                a0, a1 = keep * a0, keep * a1
                ca = a0 + a1
                cu = near if q == 9 else a0 + a1 * qu
                cd = near if q == 6 else a0 + a1 * qd
                co = a0 + a1 * qo
                cb = a0 + a1 * qb
                cl = a0 + a1 * ql
                cr = a0 + a1 * qn
            ca = 2.4 * ca
            cu, cd, co, cb, cl, cr = cu * gu, cd * gd, co * go, cb * gb, cl * g_l, cr * g_r
            for c in range(COMPS):
                total = ca * b_t[c, r] + cu * x0[c, r, 8:24, :]
                total = total + (cd * x0[c, r + 2, 8:24, :] + co * x0[c, r + 1, 7:23, :])
                total = total + (cb * x0[c, r + 1, 9:25, :] + cl * moved[q, c, :, :LANES])
                loc_t[c, r] = total + cr * moved[q, c, :, LANES:]
        part = pl.ds(s * SX, SX)
        for d in range(DEPTH):
            pltpu.make_async_copy(
                loc_t.at[:, part, d, :], loc_n.at[:, d, part, :], loc_sem
            ).start()
        return 0

    lax.fori_loop(0, SUBS // 2, second_block, 0)

    for o in range(1, nx):
        one(o, gx).wait_send()
        one(o, lax.rem(gx + nx - o, nx)).wait_recv()
    joined = parts[0]
    for i in range(1, nx):
        joined = joined + parts[i]
    coarse[gy] = joined
    for o in range(1, ny):
        two(o, gy).start()
    lax.fori_loop(SUBS // 2, SUBS, second_block, 0)

    pltpu.make_async_copy(pieces, pieces, g_sem).wait()
    for o in range(1, ny):
        two(o, gy).wait_send()
        two(o, lax.rem(gy + ny - o, ny)).wait_recv()
    for s in range(SUBS):
        fetched = jnp.zeros((KMAX, LANES), F32)
        for l in range(NLIST):
            n = table_ref[s, 0, l]
            tile = jnp.where(lane8 == (n >> 4), coarse[n & (ny - 1)], 0.0)
            fetched = jnp.where(lane8 == l, jnp.sum(tile, axis=1, keepdims=True), fetched)
        acc = jnp.zeros((KMAX, NLIST), F32)
        for b in range(KMAX):
            acc = acc + pieces[s, b] * fetched[b : b + 1, :NLIST]
        answer = jnp.broadcast_to(jnp.sum(acc, axis=1, keepdims=True), (KMAX, LANES))
        answer = jnp.where(sub8 < tally_ref[0, s], answer, 0.0)
        sol[s] = answer.astype(BF16).astype(F32)
    pltpu.make_async_copy(loc_n, loc_n, loc_sem).wait()


def finish(loc_n, v_n, sol, out_hbm, out_v, out_sem):
    def out_copy(s):
        part = pl.ds(s * SX, SX)
        return pltpu.make_async_copy(out_v.at[:, :, part], out_hbm.at[:, :, part], out_sem.at[s])

    for s in range(SUBS):
        part = slice(s * SX, s * SX + SX)
        weights = [jnp.broadcast_to(sol[s, k : k + 1, :], (SX, LANES)) for k in range(KMAX)]

        def prolong(i, _):
            for j in range(4):
                d = i * 4 + j
                for c in range(COMPS):
                    total = loc_n[c, d, part, :]
                    for k in range(KMAX):
                        total = total + v_n[k, c, d, part, :].astype(F32) * weights[k]
                    out_v[c, d, part, :] = total
            return 0

        lax.fori_loop(0, DEPTH // 4, prolong, 0)
        out_copy(s).start()
    for s in range(SUBS):
        out_copy(s).wait()


def local(
    equation_misfit,
    thermal_excess,
    spanning_vectors,
    global_solve_pieces,
    influencing_partition_table,
    spanning_vector_tally,
):
    nx, ny = lax.axis_size("gx"), lax.axis_size("gy")
    hbm = pl.BlockSpec(memory_space=pltpu.HBM)
    smem = pl.BlockSpec(memory_space=pltpu.SMEM)
    vmem = pl.BlockSpec(memory_space=pltpu.VMEM)
    plane = (DEPTH, LANES)
    wide = (DEPTH, 2 * LANES)
    cuts = 2 * SUBS

    def f32(*shape):
        return pltpu.VMEM(shape, F32)

    def low(*shape):
        return pltpu.VMEM(shape, BF16)

    dma = pltpu.SemaphoreType.DMA
    scratch = [
        f32(ROWS, *plane),
        f32(COMPS, ROWS, *plane),
        f32(COMPS, DEPTH, ROWS, LANES),
        f32(SUBS, KMAX, KMAX, NLIST),
        f32(ROWS + 4, 32, LANES),
        f32(ROWS + 2, *wide),
        f32(8, *plane),
        f32(2, 8, *plane),
        f32(2, 5, *plane),
        f32(2, 5, *plane),
        f32(4, *plane),
        f32(2, *plane),
        f32(2, COMPS, *plane),
        f32(2, *plane),
        low(2 * LANES, 2 * LANES),
        f32(COMPS, ROWS + 2, 32, LANES),
        low(ROWS, COMPS, *wide),
        f32(SX, COMPS, *wide),
        f32(ROWS, *plane),
        f32(ROWS, *plane),
        f32(ROWS + 2, 32, LANES),
        f32(ROWS, *plane),
        f32(ROWS, *plane),
        f32(2, cuts, *plane),
        f32(2, cuts, 32, LANES),
        f32(2, cuts, *wide),
        f32(COMPS, ROWS, *plane),
        f32(SUBS, KMAX, SX, LANES),
        f32(nx, KMAX, LANES),
        f32(ny, KMAX, LANES),
        dma,
        dma,
        dma,
        dma,
        dma((2 * COMPS,)),
        dma,
        dma((8,)),
        dma((8,)),
        dma((nx - 1,)),
        dma((nx - 1,)),
        dma((ny - 1,)),
        dma((ny - 1,)),
    ]
    loc, vectors, sol = pl.pallas_call(
        kernel,
        out_shape=[
            pltpu.VMEM(equation_misfit.shape, F32),
            pltpu.VMEM(spanning_vectors.shape, BF16),
            pltpu.VMEM((SUBS, KMAX, LANES), F32),
        ],
        in_specs=[hbm, hbm, hbm, hbm, smem, smem],
        out_specs=[vmem] * 3,
        scratch_shapes=scratch,
        compiler_params=pltpu.CompilerParams(
            collective_id=0, has_side_effects=True, vmem_limit_bytes=52 * 2**20
        ),
        name="schwarz",
    )(
        equation_misfit,
        thermal_excess,
        spanning_vectors,
        jnp.transpose(global_solve_pieces, (0, 1, 3, 4, 2)),
        influencing_partition_table,
        jnp.transpose(spanning_vector_tally),
    )
    return pl.pallas_call(
        finish,
        out_shape=jax.ShapeDtypeStruct(equation_misfit.shape, F32),
        in_specs=[vmem] * 3,
        out_specs=hbm,
        scratch_shapes=[f32(COMPS, DEPTH, ROWS, LANES), dma((SUBS,))],
        compiler_params=pltpu.CompilerParams(vmem_limit_bytes=40 * 2**20),
        name="finish",
    )(loc, vectors, sol)


def solution(mesh):
    return jax.shard_map(
        local,
        mesh=mesh,
        in_specs=(
            P(None, None, "gx", "gy"),
            P(None, "gx", "gy"),
            P(None, None, None, "gx", "gy"),
            P("gx", "gy", None, None, None),
            P("gx", "gy", None),
            P("gx", "gy"),
        ),
        out_specs=P(None, None, "gx", "gy"),
        check_vma=False,
    )
```

```python
import jax
import jax.numpy as jnp
from jax import lax
from jax.experimental import pallas as pl
from jax.experimental.pallas import tpu as pltpu
from jax.sharding import PartitionSpec as P

F32 = jnp.float32
BF16 = jnp.bfloat16
MESH = pl.DeviceIdType.MESH

COMPS = 3
DEPTH = 16
ROWS = 64
LANES = 128
SUBS = 4
SX = 16
KMAX = 8
NLIST = 9

MASS_TERM = 0.05
RELAX_WEIGHT = 0.8
ARRHENIUS_FACTOR = 6.0


def kernel(
    b_hbm,
    te_hbm,
    v_hbm,
    g_hbm,
    table_ref,
    tally_ref,
    loc_n,
    v_n,
    sol,
    te_t,
    b_t,
    b_n,
    pieces,
    shear,
    shear_lr,
    edge_own,
    edge_got,
    rows_own,
    rows_got,
    corner_got,
    edge_m,
    edge_x,
    edge_q,
    shift,
    x0,
    lhs,
    moved,
    s0,
    s1,
    q1,
    gl,
    gr,
    sr,
    qr,
    qr_lr,
    loc_t,
    sums,
    parts,
    coarse,
    te_sem,
    bt_sem,
    bn_sem,
    g_sem,
    v_sem,
    loc_sem,
    halo_send,
    halo_recv,
    one_send,
    one_recv,
    two_send,
    two_recv,
):
    gx = lax.axis_index("gx")
    gy = lax.axis_index("gy")
    nx = lax.axis_size("gx")
    ny = lax.axis_size("gy")
    up, down = lax.rem(gx + nx - 1, nx), lax.rem(gx + 1, nx)
    left, right = lax.rem(gy + ny - 1, ny), lax.rem(gy + 1, ny)

    for d in range(DEPTH):
        pltpu.make_async_copy(te_hbm.at[d], te_t.at[:, d, :], te_sem).start()
    for d in range(DEPTH):
        pltpu.make_async_copy(b_hbm.at[:, d], b_t.at[:, :, d, :], bt_sem).start()
    pltpu.make_async_copy(b_hbm, b_n, bn_sem).start()
    half = DEPTH // 2

    def v_copy(i):
        part = pl.ds((i % 2) * half, half)
        return pltpu.make_async_copy(
            v_hbm.at[:, i // 2, part], v_n.at[:, i // 2, part], v_sem.at[i]
        )

    for i in range(2 * COMPS):
        v_copy(i).start()
    for a in range(KMAX):
        pltpu.make_async_copy(g_hbm.at[:, 0, a], pieces.at[:, :, a, :], g_sem).start()

    barrier = pltpu.get_barrier_semaphore()
    for o in range(1, nx):
        pl.semaphore_signal(barrier, 1, device_id=(lax.rem(gx + o, nx), gy), device_id_type=MESH)
    for o in range(1, ny):
        pl.semaphore_signal(barrier, 1, device_id=(gx, lax.rem(gy + o, ny)), device_id_type=MESH)
    for px in (up, down):
        for py in (left, right):
            pl.semaphore_signal(barrier, 1, device_id=(px, py), device_id_type=MESH)

    lane = lax.broadcasted_iota(jnp.int32, (DEPTH, LANES), 1)
    sub = lax.broadcasted_iota(jnp.int32, (DEPTH, LANES), 0)

    wi = lax.broadcasted_iota(jnp.int32, (2 * LANES, 2 * LANES), 0)
    wj = lax.broadcasted_iota(jnp.int32, (2 * LANES, 2 * LANES), 1)
    own, to_left = wi < LANES, wj < LANES
    hit = (
        (own & to_left & (wi == wj - 1))
        | (own & ~to_left & (wi == wj - LANES + 1))
        | (~own & ((wi & 3) == 3) & (wj == 0))
        | (~own & ((wi & 3) == 0) & (wj == 2 * LANES - 1))
    )
    shift[...] = jnp.where(hit, 1.0, 0.0).astype(BF16)

    zeros = jnp.zeros((COMPS, 8, LANES), F32)
    zero = jnp.zeros((8, LANES), F32)

    def clear(p, _):
        x0[:, p, 0:8, :] = zeros
        x0[:, p, 24:32, :] = zeros
        q1[p, 0:8, :] = zero
        q1[p, 24:32, :] = zero
        return 0

    lax.fori_loop(0, ROWS + 2, clear, 0)

    def clear_cut(p, _):
        for v in range(2):
            qr[v, p, 0:8, :] = zero
            qr[v, p, 24:32, :] = zero
        return 0

    lax.fori_loop(0, 2 * SUBS, clear_cut, 0)
    sums[...] = jnp.zeros(sums.shape, F32)

    def put_shear(p, m):
        shear[p, 8:24, :] = m
        shear[p, 7:8, :] = m[0:1]
        shear[p, 24:25, :] = m[15:16]

    pltpu.make_async_copy(te_t, te_t, te_sem).wait()

    def make_shear(i, _):
        for j in range(4):
            r = i * 4 + j
            m = 1.0 / (1.0 + jnp.exp(ARRHENIUS_FACTOR * (1.0 - 1.0 / te_t[r])))
            put_shear(r + 2, m)
        return 0

    lax.fori_loop(0, ROWS // 4, make_shear, 0)
    pltpu.make_async_copy(b_t, b_t, bt_sem).wait()

    slot = ((lane + 2) & (LANES - 1)) >> 2

    def pack(i, held):
        for j in range(4):
            rr = i * 4 + j
            here = slot == rr
            new = []
            for f in range(4):
                for h in range(2):
                    r = rr + 32 * h
                    val = shear[r + 2, 8:24, :] if f == 0 else b_t[f - 1, r]
                    new.append(jnp.where(here, pltpu.roll(val, 4 * rr, 1), held[f * 2 + h]))
            held = tuple(new)
        return held

    packed = lax.fori_loop(0, 8, pack, tuple(jnp.zeros((DEPTH, LANES), F32) for _ in range(8)))
    for i in range(8):
        edge_own[i] = packed[i]
    for side, (near, next_) in enumerate(((0, 1), (ROWS - 1, ROWS - 2))):
        rows_own[side, 0] = shear[near + 2, 8:24, :]
        rows_own[side, 1] = shear[next_ + 2, 8:24, :]
        for c in range(COMPS):
            rows_own[side, 2 + c] = b_t[c, near]

    pl.semaphore_wait(barrier, (nx - 1) + (ny - 1) + 4)

    def halo(i, src, dst, px, py):
        return pltpu.make_async_remote_copy(
            src_ref=src,
            dst_ref=dst,
            send_sem=halo_send.at[i],
            recv_sem=halo_recv.at[i],
            device_id=(px, py),
            device_id_type=MESH,
        )

    halos = [
        halo(0, rows_own.at[0], rows_got.at[1], up, gy),
        halo(1, rows_own.at[1], rows_got.at[0], down, gy),
        halo(2, edge_own, edge_got.at[1], gx, left),
        halo(3, edge_own, edge_got.at[0], gx, right),
        halo(4, rows_own.at[0, 0], corner_got.at[3], up, left),
        halo(5, rows_own.at[0, 0], corner_got.at[2], up, right),
        halo(6, rows_own.at[1, 0], corner_got.at[1], down, left),
        halo(7, rows_own.at[1, 0], corner_got.at[0], down, right),
    ]
    for copy in halos:
        copy.start()

    pltpu.make_async_copy(b_n, b_n, bn_sem).wait()
    for i in range(2 * COMPS):
        v_copy(i).wait()

        def restrict(s, _):
            part = pl.ds(pl.multiple_of(s * SX, SX), SX)
            c = i // 2
            accs = [sums[s, k] for k in range(KMAX)]
            for j in range(half):
                d = (i % 2) * half + j
                low = b_n[c, d, part, :].astype(BF16).astype(F32)
                for k in range(KMAX):
                    accs[k] = accs[k] + v_n[k, c, d, part, :].astype(F32) * low
            for k in range(KMAX):
                sums[s, k] = accs[k]
            return 0

        lax.fori_loop(0, SUBS, restrict, 0)
    lane8 = lax.broadcasted_iota(jnp.int32, (KMAX, LANES), 1)
    sub8 = lax.broadcasted_iota(jnp.int32, (KMAX, LANES), 0)
    rhs = jnp.zeros((KMAX, LANES), F32)
    for s in range(SUBS):
        total = jnp.sum(jnp.sum(sums[s], axis=1), axis=1, keepdims=True)
        total = jnp.where(sub8 < tally_ref[0, s], total, 0.0)
        rhs = jnp.where(lane8 == gx * SUBS + s, total, rhs)
    parts[gx] = rhs

    def one(o, who):
        return pltpu.make_async_remote_copy(
            src_ref=parts.at[who],
            dst_ref=parts.at[who],
            send_sem=one_send.at[o - 1],
            recv_sem=one_recv.at[o - 1],
            device_id=(lax.rem(gx + o, nx), gy),
            device_id_type=MESH,
        )

    def two(o, who):
        return pltpu.make_async_remote_copy(
            src_ref=coarse.at[who],
            dst_ref=coarse.at[who],
            send_sem=two_send.at[o - 1],
            recv_sem=two_recv.at[o - 1],
            device_id=(gx, lax.rem(gy + o, ny)),
            device_id_type=MESH,
        )

    for o in range(1, nx):
        one(o, gx).start()

    for copy in halos:
        copy.wait()

    def flag(cond):
        return jnp.where(cond, 1.0, 0.0).astype(F32)

    k_up, k_down = flag(gx > 0), flag(gx < nx - 1)
    k_left, k_right = flag(gy > 0), flag(gy < ny - 1)
    put_shear(1, rows_got[0, 0] * k_up)
    put_shear(0, rows_got[0, 1] * k_up)
    put_shear(ROWS + 2, rows_got[1, 0] * k_down)
    put_shear(ROWS + 3, rows_got[1, 1] * k_down)
    from_left = (lane & 3) >= 2
    got = [
        jnp.where(from_left, edge_got[0, i] * k_left, edge_got[1, i] * k_right) for i in range(8)
    ]
    corner_up = jnp.where(
        lane == LANES - 1, corner_got[0] * (k_up * k_left), corner_got[1] * (k_up * k_right)
    )
    corner_down = jnp.where(
        lane == LANES - 1, corner_got[2] * (k_down * k_left), corner_got[3] * (k_down * k_right)
    )
    first, last = slot == 0, slot == 31
    back4 = LANES - 4
    ups = [
        jnp.where(first, corner_up, pltpu.roll(got[0], 4, 1)),
        jnp.where(first, pltpu.roll(got[0], 4, 1), pltpu.roll(got[1], 4, 1)),
    ]
    downs = [
        jnp.where(last, pltpu.roll(got[1], back4, 1), pltpu.roll(got[0], back4, 1)),
        jnp.where(last, pltpu.roll(corner_down, back4, 1), pltpu.roll(got[1], back4, 1)),
    ]
    spot = slot & (SX - 1)
    for h in range(2):
        m, mine = got[h], edge_own[h]
        sides = jnp.where(
            (lane & 3) == 3,
            pltpu.roll(m, 1, 1) + pltpu.roll(mine, LANES - 1, 1),
            pltpu.roll(m, LANES - 1, 1) + pltpu.roll(mine, 1, 1),
        )
        over = jnp.where(sub == 0, m, pltpu.roll(m, 1, 0))
        under = jnp.where(sub == DEPTH - 1, m, pltpu.roll(m, DEPTH - 1, 0))
        diag = MASS_TERM + 3.0 * m + 0.5 * (ups[h] + downs[h] + sides + over + under)
        cut = jnp.where(spot == 7, m - downs[h], jnp.where(spot == 8, m - ups[h], 0.0))
        scale = RELAX_WEIGHT / diag
        edge_m[h] = m
        edge_q[h] = diag / (diag + 0.5 * cut)
        for c in range(COMPS):
            edge_x[h, c] = scale * got[2 + 2 * c + h]

    for o in range(1, nx):
        one(o, gx).wait_send()
        one(o, lax.rem(gx + nx - o, nx)).wait_recv()
    joined = parts[0]
    for i in range(1, nx):
        joined = joined + parts[i]
    coarse[gy] = joined
    for o in range(1, ny):
        two(o, gy).start()
    lane3 = lax.broadcasted_iota(jnp.int32, (SX, DEPTH, LANES), 2)
    plane3 = lax.broadcasted_iota(jnp.int32, (SX, DEPTH, LANES), 0)
    pair3 = ((lane3 + 1) & (LANES - 1)) >> 1
    pair = ((lane + 1) & (LANES - 1)) >> 1

    def shear_sides(s, _):
        base = s * SX
        mine = shear[pl.ds(base + 2, SX), 8:24, :]
        theirs = jnp.where(pair3 == 2 * ((plane3 + base) & 31), edge_m[s // 2][None], 0.0)
        both = jnp.concatenate([mine, theirs], axis=2).astype(BF16)
        result = jnp.dot(both.reshape(SX * DEPTH, 2 * LANES), shift[...], preferred_element_type=F32)
        shear_lr[pl.ds(base + 1, SX)] = result.reshape(SX, DEPTH, 2 * LANES)
        return 0

    lax.fori_loop(0, SUBS, shear_sides, 0)
    ends = jnp.concatenate(
        [
            jnp.concatenate([shear[1, 8:24, :], jnp.where(pair == 0, corner_up, 0.0)], axis=1),
            jnp.concatenate([shear[ROWS + 2, 8:24, :], jnp.where(pair == 0, corner_down, 0.0)], axis=1),
        ],
        axis=0,
    ).astype(BF16)
    result = jnp.dot(ends, shift[...], preferred_element_type=F32)
    shear_lr[0] = result[:DEPTH]
    shear_lr[ROWS + 1] = result[DEPTH:]

    def first_sweep(p):
        m = shear[p + 1, 8:24, :]
        mu, md = shear[p, 8:24, :], shear[p + 2, 8:24, :]
        mo, mb = shear[p + 1, 7:23, :], shear[p + 1, 9:25, :]
        ml, mr = shear_lr[p, :, :LANES], shear_lr[p, :, LANES:]
        diag = MASS_TERM + 3.0 * m + 0.5 * ((mu + md) + (ml + mr) + (mo + mb))
        cut = 0.5 * jnp.where(lane == 7, m - mr, jnp.where(lane == 120, m - ml, 0.0))
        return m, mu, md, ml, mr, diag, cut

    ratio = 1.0 / RELAX_WEIGHT
    for p, side, keep in ((0, 0, k_up), (ROWS + 1, 1, k_down)):
        _, _, _, _, _, diag, cut = first_sweep(p)
        x0[:, p, 8:24, :] = (RELAX_WEIGHT / diag) * (rows_got[side, 2:5] * keep)
        q1[p, 8:24, :] = diag / (diag + cut)

    def sweep_block(s, _):
        for q in range(SX):
            r = s * SX + q
            m, mu, md, ml, mr, diag, cut = first_sweep(r + 1)
            gl[r] = m + ml
            gr[r] = m + mr
            scale = RELAX_WEIGHT / diag
            cut_scale = RELAX_WEIGHT / (diag + cut)
            ratio_diag = ratio * diag
            s0[r] = scale
            s1[r] = cut_scale
            q1[r + 1, 8:24, :] = cut_scale * ratio_diag
            x = scale * b_t[:, r]
            x0[:, r + 1, 8:24, :] = x
            here = pair == 2 * (r & 31)
            lhs[r, :, :, :LANES] = x.astype(BF16)
            lhs[r, :, :, LANES:] = jnp.where(here, edge_x[s // 2], 0.0).astype(BF16)
            if q in (7, 8):
                e = s * 2 + (q - 7)
                diag = diag + 0.5 * (m - (md if q == 7 else mu))
                for v, dg in ((0, diag), (1, diag + cut)):
                    scale = RELAX_WEIGHT / dg
                    sr[v, e] = scale
                    qr[v, e, 8:24, :] = scale * ratio_diag
        return 0

    lax.fori_loop(0, SUBS, sweep_block, 0)
    for v in range(2):
        rows = []
        for e in range(2 * SUBS):
            r = (e // 2) * SX + 7 + e % 2
            theirs = jnp.where(pair == 2 * (r & 31), edge_q[r // 32], 0.0)
            rows.append(jnp.concatenate([qr[v, e, 8:24, :], theirs], axis=1))
        rows = jnp.concatenate(rows, axis=0).astype(BF16)
        result = jnp.dot(rows, shift[...], preferred_element_type=F32)
        qr_lr[v] = result.reshape(2 * SUBS, DEPTH, 2 * LANES)

    edge_lo, edge_hi = lane < 8, lane >= 120
    w0 = jnp.where(edge_lo | edge_hi, 0.25, 0.5).astype(F32)
    w1 = jnp.where(edge_lo, 0.25 * k_left, jnp.where(edge_hi, 0.25 * k_right, 0.0)).astype(F32)
    few = 4

    def second_block(s, _):
        for j in range(SX // few):
            rows = lhs[pl.ds(s * SX + j * few, few)].reshape(few * COMPS * DEPTH, 2 * LANES)
            result = jnp.dot(rows, shift[...], preferred_element_type=F32)
            moved[j * few : (j + 1) * few] = result.reshape(few, COMPS, DEPTH, 2 * LANES)
        for q in range(SX):
            r = s * SX + q
            m = shear[r + 2, 8:24, :]
            gu, gd = m + shear[r + 1, 8:24, :], m + shear[r + 3, 8:24, :]
            go, gb = m + shear[r + 2, 7:23, :], m + shear[r + 2, 9:25, :]
            g_l, g_r = gl[r], gr[r]
            if q < 8:
                keep = jnp.where((gx == 0) & (s == 0), 0.5, 1.0)
            else:
                keep = jnp.where((gx == nx - 1) & (s == SUBS - 1), 0.5, 1.0)
            rest = keep - 0.5
            a0, a1 = w0 * s0[r], w1 * s1[r]
            qu, qd = q1[r, 8:24, :], q1[r + 2, 8:24, :]
            qo, qb = q1[r + 1, 7:23, :], q1[r + 1, 9:25, :]
            qm = q1[r + 1, 8:24, :]
            ql = jnp.where(lane == 121, pltpu.roll(qm, 1, 1), 1.0)
            ql = jnp.where(lane == 120, 0.0, ql)
            qn = jnp.where(lane == 6, pltpu.roll(qm, LANES - 1, 1), 1.0)
            qn = jnp.where(lane == 7, 0.0, qn)
            e = s * 2 + (0 if q < 8 else 1)
            if q in (7, 8):
                r0, r1 = rest * w0 * sr[0, e], rest * w1 * sr[1, e]
                a0, a1 = 0.5 * a0, 0.5 * a1
                ca = a0 + a1 + r0 + r1
                cu = (a0 + r0) + (a1 + r1) * qu if q == 7 else a0 + a1 * qu
                cd = (a0 + r0) + (a1 + r1) * qd if q == 8 else a0 + a1 * qd
                co = (a0 + a1 * qo) + (r0 * qr[0, e, 7:23, :] + r1 * qr[1, e, 7:23, :])
                cb = (a0 + a1 * qb) + (r0 * qr[0, e, 9:25, :] + r1 * qr[1, e, 9:25, :])
                r1l, r1r = jnp.where(lane == 120, 0.0, r1), jnp.where(lane == 7, 0.0, r1)
                cl = (a0 + a1 * ql) + (r0 * qr_lr[0, e, :, :LANES] + r1l * qr_lr[1, e, :, :LANES])
                cr = (a0 + a1 * qn) + (r0 * qr_lr[0, e, :, LANES:] + r1r * qr_lr[1, e, :, LANES:])
            else:
                if q in (6, 9):
                    k0 = 0.5 + rest * qr[0, e, 8:24, :]
                    near = a0 * k0
                    qx = qd if q == 6 else qu
                    near = near + a1 * (0.5 * qx + rest * qr[1, e, 8:24, :])
                a0, a1 = keep * a0, keep * a1
                ca = a0 + a1
                cu = near if q == 9 else a0 + a1 * qu
                cd = near if q == 6 else a0 + a1 * qd
                co = a0 + a1 * qo
                cb = a0 + a1 * qb
                cl = a0 + a1 * ql
                cr = a0 + a1 * qn
            ca = 2.4 * ca
            cu, cd, co, cb, cl, cr = cu * gu, cd * gd, co * go, cb * gb, cl * g_l, cr * g_r
            for c in range(COMPS):
                total = ca * b_t[c, r] + cu * x0[c, r, 8:24, :]
                total = total + (cd * x0[c, r + 2, 8:24, :] + co * x0[c, r + 1, 7:23, :])
                total = total + (cb * x0[c, r + 1, 9:25, :] + cl * moved[q, c, :, :LANES])
                loc_t[c, r] = total + cr * moved[q, c, :, LANES:]
        part = pl.ds(s * SX, SX)
        for d in range(DEPTH):
            pltpu.make_async_copy(
                loc_t.at[:, part, d, :], loc_n.at[:, d, part, :], loc_sem
            ).start()
        return 0


    lax.fori_loop(0, SUBS, second_block, 0)

    pltpu.make_async_copy(pieces, pieces, g_sem).wait()
    for o in range(1, ny):
        two(o, gy).wait_send()
        two(o, lax.rem(gy + ny - o, ny)).wait_recv()
    for s in range(SUBS):
        fetched = jnp.zeros((KMAX, LANES), F32)
        for l in range(NLIST):
            n = table_ref[s, 0, l]
            tile = jnp.where(lane8 == (n >> 4), coarse[n & (ny - 1)], 0.0)
            fetched = jnp.where(lane8 == l, jnp.sum(tile, axis=1, keepdims=True), fetched)
        acc = jnp.zeros((KMAX, NLIST), F32)
        for b in range(KMAX):
            acc = acc + pieces[s, b] * fetched[b : b + 1, :NLIST]
        answer = jnp.broadcast_to(jnp.sum(acc, axis=1, keepdims=True), (KMAX, LANES))
        answer = jnp.where(sub8 < tally_ref[0, s], answer, 0.0)
        sol[s] = answer.astype(BF16).astype(F32)
    pltpu.make_async_copy(loc_n, loc_n, loc_sem).wait()


def finish(loc_n, v_n, sol, out_hbm, out_v, out_sem):
    def out_copy(s):
        part = pl.ds(s * SX, SX)
        return pltpu.make_async_copy(out_v.at[:, :, part], out_hbm.at[:, :, part], out_sem.at[s])

    for s in range(SUBS):
        part = slice(s * SX, s * SX + SX)
        weights = [jnp.broadcast_to(sol[s, k : k + 1, :], (SX, LANES)) for k in range(KMAX)]

        def prolong(i, _):
            for j in range(4):
                d = i * 4 + j
                for c in range(COMPS):
                    total = loc_n[c, d, part, :]
                    for k in range(KMAX):
                        total = total + v_n[k, c, d, part, :].astype(F32) * weights[k]
                    out_v[c, d, part, :] = total
            return 0

        lax.fori_loop(0, DEPTH // 4, prolong, 0)
        out_copy(s).start()
    for s in range(SUBS):
        out_copy(s).wait()


def local(
    equation_misfit,
    thermal_excess,
    spanning_vectors,
    global_solve_pieces,
    influencing_partition_table,
    spanning_vector_tally,
):
    nx, ny = lax.axis_size("gx"), lax.axis_size("gy")
    hbm = pl.BlockSpec(memory_space=pltpu.HBM)
    smem = pl.BlockSpec(memory_space=pltpu.SMEM)
    vmem = pl.BlockSpec(memory_space=pltpu.VMEM)
    plane = (DEPTH, LANES)
    wide = (DEPTH, 2 * LANES)
    cuts = 2 * SUBS

    def f32(*shape):
        return pltpu.VMEM(shape, F32)

    def low(*shape):
        return pltpu.VMEM(shape, BF16)

    dma = pltpu.SemaphoreType.DMA
    scratch = [
        f32(ROWS, *plane),
        f32(COMPS, ROWS, *plane),
        f32(COMPS, DEPTH, ROWS, LANES),
        f32(SUBS, KMAX, KMAX, NLIST),
        f32(ROWS + 4, 32, LANES),
        f32(ROWS + 2, *wide),
        f32(8, *plane),
        f32(2, 8, *plane),
        f32(2, 5, *plane),
        f32(2, 5, *plane),
        f32(4, *plane),
        f32(2, *plane),
        f32(2, COMPS, *plane),
        f32(2, *plane),
        low(2 * LANES, 2 * LANES),
        f32(COMPS, ROWS + 2, 32, LANES),
        low(ROWS, COMPS, *wide),
        f32(SX, COMPS, *wide),
        f32(ROWS, *plane),
        f32(ROWS, *plane),
        f32(ROWS + 2, 32, LANES),
        f32(ROWS, *plane),
        f32(ROWS, *plane),
        f32(2, cuts, *plane),
        f32(2, cuts, 32, LANES),
        f32(2, cuts, *wide),
        f32(COMPS, ROWS, *plane),
        f32(SUBS, KMAX, SX, LANES),
        f32(nx, KMAX, LANES),
        f32(ny, KMAX, LANES),
        dma,
        dma,
        dma,
        dma,
        dma((2 * COMPS,)),
        dma,
        dma((8,)),
        dma((8,)),
        dma((nx - 1,)),
        dma((nx - 1,)),
        dma((ny - 1,)),
        dma((ny - 1,)),
    ]
    loc, vectors, sol = pl.pallas_call(
        kernel,
        out_shape=[
            pltpu.VMEM(equation_misfit.shape, F32),
            pltpu.VMEM(spanning_vectors.shape, BF16),
            pltpu.VMEM((SUBS, KMAX, LANES), F32),
        ],
        in_specs=[hbm, hbm, hbm, hbm, smem, smem],
        out_specs=[vmem] * 3,
        scratch_shapes=scratch,
        compiler_params=pltpu.CompilerParams(
            collective_id=0, has_side_effects=True, vmem_limit_bytes=52 * 2**20
        ),
        name="schwarz",
    )(
        equation_misfit,
        thermal_excess,
        spanning_vectors,
        jnp.transpose(global_solve_pieces, (0, 1, 3, 4, 2)),
        influencing_partition_table,
        jnp.transpose(spanning_vector_tally),
    )
    return pl.pallas_call(
        finish,
        out_shape=jax.ShapeDtypeStruct(equation_misfit.shape, F32),
        in_specs=[vmem] * 3,
        out_specs=hbm,
        scratch_shapes=[f32(COMPS, DEPTH, ROWS, LANES), dma((SUBS,))],
        compiler_params=pltpu.CompilerParams(vmem_limit_bytes=40 * 2**20),
        name="finish",
    )(loc, vectors, sol)


def solution(mesh):
    return jax.shard_map(
        local,
        mesh=mesh,
        in_specs=(
            P(None, None, "gx", "gy"),
            P(None, "gx", "gy"),
            P(None, None, None, "gx", "gy"),
            P("gx", "gy", None, None, None),
            P("gx", "gy", None),
            P("gx", "gy"),
        ),
        out_specs=P(None, None, "gx", "gy"),
        check_vma=False,
    )
```

```python
import jax
import jax.numpy as jnp
from jax import lax
from jax.experimental import pallas as pl
from jax.experimental.pallas import tpu as pltpu
from jax.sharding import PartitionSpec as P

F32 = jnp.float32
BF16 = jnp.bfloat16
MESH = pl.DeviceIdType.MESH

COMPS = 3
DEPTH = 16
ROWS = 64
LANES = 128
SUBS = 4
SX = 16
KMAX = 8
NLIST = 9

MASS_TERM = 0.05
RELAX_WEIGHT = 0.8
ARRHENIUS_FACTOR = 6.0


def kernel(
    b_hbm,
    te_hbm,
    v_hbm,
    g_hbm,
    table_ref,
    tally_ref,
    loc_n,
    v_n,
    sol,
    te_t,
    b_t,
    b_n,
    pieces,
    shear,
    shear_lr,
    edge_own,
    edge_got,
    rows_own,
    rows_got,
    corner_got,
    edge_m,
    edge_x,
    edge_q,
    edge_s,
    end_s,
    shift,
    x0,
    lhs,
    moved,
    s0,
    s1,
    q1,
    gl,
    gr,
    sr,
    qr,
    qr_lr,
    loc_t,
    sums,
    parts,
    coarse,
    te_sem,
    bt_sem,
    bn_sem,
    g_sem,
    v_sem,
    loc_sem,
    halo_send,
    halo_recv,
    one_send,
    one_recv,
    two_send,
    two_recv,
):
    gx = lax.axis_index("gx")
    gy = lax.axis_index("gy")
    nx = lax.axis_size("gx")
    ny = lax.axis_size("gy")
    up, down = lax.rem(gx + nx - 1, nx), lax.rem(gx + 1, nx)
    left, right = lax.rem(gy + ny - 1, ny), lax.rem(gy + 1, ny)

    for d in range(DEPTH):
        pltpu.make_async_copy(te_hbm.at[d], te_t.at[:, d, :], te_sem).start()
    pltpu.make_async_copy(b_hbm, b_n, bn_sem).start()
    half = DEPTH // 2

    def v_copy(i):
        part = pl.ds((i % 2) * half, half)
        return pltpu.make_async_copy(
            v_hbm.at[:, i // 2, part], v_n.at[:, i // 2, part], v_sem.at[i]
        )

    for i in range(2 * COMPS):
        v_copy(i).start()
    for d in range(DEPTH):
        pltpu.make_async_copy(b_hbm.at[:, d], b_t.at[:, :, d, :], bt_sem).start()
    for a in range(KMAX):
        pltpu.make_async_copy(g_hbm.at[:, 0, a], pieces.at[:, :, a, :], g_sem).start()

    barrier = pltpu.get_barrier_semaphore()
    for o in range(1, nx):
        pl.semaphore_signal(barrier, 1, device_id=(lax.rem(gx + o, nx), gy), device_id_type=MESH)
    for o in range(1, ny):
        pl.semaphore_signal(barrier, 1, device_id=(gx, lax.rem(gy + o, ny)), device_id_type=MESH)
    for px in (up, down):
        for py in (left, right):
            pl.semaphore_signal(barrier, 1, device_id=(px, py), device_id_type=MESH)

    lane = lax.broadcasted_iota(jnp.int32, (DEPTH, LANES), 1)
    sub = lax.broadcasted_iota(jnp.int32, (DEPTH, LANES), 0)

    wi = lax.broadcasted_iota(jnp.int32, (2 * LANES, 2 * LANES), 0)
    wj = lax.broadcasted_iota(jnp.int32, (2 * LANES, 2 * LANES), 1)
    own, to_left = wi < LANES, wj < LANES
    hit = (
        (own & to_left & (wi == wj - 1))
        | (own & ~to_left & (wi == wj - LANES + 1))
        | (~own & ((wi & 3) == 3) & (wj == 0))
        | (~own & ((wi & 3) == 0) & (wj == 2 * LANES - 1))
    )
    shift[...] = jnp.where(hit, 1.0, 0.0).astype(BF16)

    zeros = jnp.zeros((COMPS, 8, LANES), F32)
    zero = jnp.zeros((8, LANES), F32)

    def clear(p, _):
        x0[:, p, 0:8, :] = zeros
        x0[:, p, 24:32, :] = zeros
        q1[p, 0:8, :] = zero
        q1[p, 24:32, :] = zero
        return 0

    lax.fori_loop(0, ROWS + 2, clear, 0)

    def clear_cut(p, _):
        for v in range(2):
            qr[v, p, 0:8, :] = zero
            qr[v, p, 24:32, :] = zero
        return 0

    lax.fori_loop(0, 2 * SUBS, clear_cut, 0)
    sums[...] = jnp.zeros(sums.shape, F32)

    def put_shear(p, m):
        shear[p, 8:24, :] = m
        shear[p, 7:8, :] = m[0:1]
        shear[p, 24:25, :] = m[15:16]

    pltpu.make_async_copy(te_t, te_t, te_sem).wait()

    def make_shear(i, _):
        for j in range(4):
            r = i * 4 + j
            m = 1.0 / (1.0 + jnp.exp(ARRHENIUS_FACTOR * (1.0 - 1.0 / te_t[r])))
            put_shear(r + 2, m)
        return 0

    lax.fori_loop(0, ROWS // 4, make_shear, 0)

    slot = ((lane + 2) & (LANES - 1)) >> 2

    def pack(fields, step):
        def some(i, held):
            for j in range(step):
                rr = i * step + j
                here = slot == rr
                new = []
                for f in range(len(fields)):
                    for h in range(2):
                        val = fields[f](rr + 32 * h)
                        new.append(jnp.where(here, pltpu.roll(val, 4 * rr, 1), held[f * 2 + h]))
                held = tuple(new)
            return held

        blank = tuple(jnp.zeros((DEPTH, LANES), F32) for _ in range(2 * len(fields)))
        return lax.fori_loop(0, 32 // step, some, blank)

    packed = pack([lambda r: shear[r + 2, 8:24, :]], 8)
    for i in range(2):
        edge_own[i] = packed[i]
    borders = ((0, 1), (ROWS - 1, ROWS - 2))
    for side, (near, next_) in enumerate(borders):
        rows_own[side, 0] = shear[near + 2, 8:24, :]
        rows_own[side, 1] = shear[next_ + 2, 8:24, :]

    pl.semaphore_wait(barrier, (nx - 1) + (ny - 1) + 4)

    def halo(i, src, dst, px, py):
        return pltpu.make_async_remote_copy(
            src_ref=src,
            dst_ref=dst,
            send_sem=halo_send.at[i],
            recv_sem=halo_recv.at[i],
            device_id=(px, py),
            device_id_type=MESH,
        )

    shears, fields, ms, bs = pl.ds(0, 2), pl.ds(2, COMPS), pl.ds(0, 2), pl.ds(2, 2 * COMPS)
    halos = [
        halo(0, rows_own.at[0, shears], rows_got.at[1, shears], up, gy),
        halo(1, rows_own.at[1, shears], rows_got.at[0, shears], down, gy),
        halo(2, edge_own.at[ms], edge_got.at[1, ms], gx, left),
        halo(3, edge_own.at[ms], edge_got.at[0, ms], gx, right),
        halo(4, rows_own.at[0, 0], corner_got.at[3], up, left),
        halo(5, rows_own.at[0, 0], corner_got.at[2], up, right),
        halo(6, rows_own.at[1, 0], corner_got.at[1], down, left),
        halo(7, rows_own.at[1, 0], corner_got.at[0], down, right),
    ]
    halos_b = [
        halo(8, rows_own.at[0, fields], rows_got.at[1, fields], up, gy),
        halo(9, rows_own.at[1, fields], rows_got.at[0, fields], down, gy),
        halo(10, edge_own.at[bs], edge_got.at[1, bs], gx, left),
        halo(11, edge_own.at[bs], edge_got.at[0, bs], gx, right),
    ]
    for copy in halos:
        copy.start()

    pltpu.make_async_copy(b_n, b_n, bn_sem).wait()
    for i in range(2 * COMPS):
        v_copy(i).wait()

        def restrict(s, _):
            part = pl.ds(pl.multiple_of(s * SX, SX), SX)
            c = i // 2
            accs = [sums[s, k] for k in range(KMAX)]
            for j in range(half):
                d = (i % 2) * half + j
                low = b_n[c, d, part, :].astype(BF16).astype(F32)
                for k in range(KMAX):
                    accs[k] = accs[k] + v_n[k, c, d, part, :].astype(F32) * low
            for k in range(KMAX):
                sums[s, k] = accs[k]
            return 0

        lax.fori_loop(0, SUBS, restrict, 0)
    lane8 = lax.broadcasted_iota(jnp.int32, (KMAX, LANES), 1)
    sub8 = lax.broadcasted_iota(jnp.int32, (KMAX, LANES), 0)
    rhs = jnp.zeros((KMAX, LANES), F32)
    for s in range(SUBS):
        total = jnp.sum(jnp.sum(sums[s], axis=1), axis=1, keepdims=True)
        total = jnp.where(sub8 < tally_ref[0, s], total, 0.0)
        rhs = jnp.where(lane8 == gx * SUBS + s, total, rhs)
    parts[gx] = rhs

    def one(o, who):
        return pltpu.make_async_remote_copy(
            src_ref=parts.at[who],
            dst_ref=parts.at[who],
            send_sem=one_send.at[o - 1],
            recv_sem=one_recv.at[o - 1],
            device_id=(lax.rem(gx + o, nx), gy),
            device_id_type=MESH,
        )

    def two(o, who):
        return pltpu.make_async_remote_copy(
            src_ref=coarse.at[who],
            dst_ref=coarse.at[who],
            send_sem=two_send.at[o - 1],
            recv_sem=two_recv.at[o - 1],
            device_id=(gx, lax.rem(gy + o, ny)),
            device_id_type=MESH,
        )

    for o in range(1, nx):
        one(o, gx).start()

    pltpu.make_async_copy(b_t, b_t, bt_sem).wait()
    packed = pack([lambda r, c=c: b_t[c, r] for c in range(COMPS)], 4)
    for i in range(2 * COMPS):
        edge_own[2 + i] = packed[i]
    for side, (near, _) in enumerate(borders):
        for c in range(COMPS):
            rows_own[side, 2 + c] = b_t[c, near]
    for copy in halos_b:
        copy.start()
    for copy in halos:
        copy.wait()

    def flag(cond):
        return jnp.where(cond, 1.0, 0.0).astype(F32)

    k_up, k_down = flag(gx > 0), flag(gx < nx - 1)
    k_left, k_right = flag(gy > 0), flag(gy < ny - 1)
    put_shear(1, rows_got[0, 0] * k_up)
    put_shear(0, rows_got[0, 1] * k_up)
    put_shear(ROWS + 2, rows_got[1, 0] * k_down)
    put_shear(ROWS + 3, rows_got[1, 1] * k_down)
    from_left = (lane & 3) >= 2

    def joined_edge(i):
        return jnp.where(from_left, edge_got[0, i] * k_left, edge_got[1, i] * k_right)

    got = [joined_edge(i) for i in range(2)]
    corner_up = jnp.where(
        lane == LANES - 1, corner_got[0] * (k_up * k_left), corner_got[1] * (k_up * k_right)
    )
    corner_down = jnp.where(
        lane == LANES - 1, corner_got[2] * (k_down * k_left), corner_got[3] * (k_down * k_right)
    )
    first, last = slot == 0, slot == 31
    back4 = LANES - 4
    ups = [
        jnp.where(first, corner_up, pltpu.roll(got[0], 4, 1)),
        jnp.where(first, pltpu.roll(got[0], 4, 1), pltpu.roll(got[1], 4, 1)),
    ]
    downs = [
        jnp.where(last, pltpu.roll(got[1], back4, 1), pltpu.roll(got[0], back4, 1)),
        jnp.where(last, pltpu.roll(corner_down, back4, 1), pltpu.roll(got[1], back4, 1)),
    ]
    spot = slot & (SX - 1)
    for h in range(2):
        m, mine = got[h], edge_own[h]
        sides = jnp.where(
            (lane & 3) == 3,
            pltpu.roll(m, 1, 1) + pltpu.roll(mine, LANES - 1, 1),
            pltpu.roll(m, LANES - 1, 1) + pltpu.roll(mine, 1, 1),
        )
        over = jnp.where(sub == 0, m, pltpu.roll(m, 1, 0))
        under = jnp.where(sub == DEPTH - 1, m, pltpu.roll(m, DEPTH - 1, 0))
        diag = MASS_TERM + 3.0 * m + 0.5 * (ups[h] + downs[h] + sides + over + under)
        cut = jnp.where(spot == 7, m - downs[h], jnp.where(spot == 8, m - ups[h], 0.0))
        edge_m[h] = m
        edge_q[h] = diag / (diag + 0.5 * cut)
        edge_s[h] = RELAX_WEIGHT / diag

    lane3 = lax.broadcasted_iota(jnp.int32, (SX, DEPTH, LANES), 2)
    plane3 = lax.broadcasted_iota(jnp.int32, (SX, DEPTH, LANES), 0)
    pair3 = ((lane3 + 1) & (LANES - 1)) >> 1
    pair = ((lane + 1) & (LANES - 1)) >> 1

    def shear_sides(s, _):
        base = s * SX
        mine = shear[pl.ds(base + 2, SX), 8:24, :]
        theirs = jnp.where(pair3 == 2 * ((plane3 + base) & 31), edge_m[s // 2][None], 0.0)
        both = jnp.concatenate([mine, theirs], axis=2).astype(BF16)
        result = jnp.dot(both.reshape(SX * DEPTH, 2 * LANES), shift[...], preferred_element_type=F32)
        shear_lr[pl.ds(base + 1, SX)] = result.reshape(SX, DEPTH, 2 * LANES)
        return 0

    lax.fori_loop(0, SUBS, shear_sides, 0)
    ends = jnp.concatenate(
        [
            jnp.concatenate([shear[1, 8:24, :], jnp.where(pair == 0, corner_up, 0.0)], axis=1),
            jnp.concatenate([shear[ROWS + 2, 8:24, :], jnp.where(pair == 0, corner_down, 0.0)], axis=1),
        ],
        axis=0,
    ).astype(BF16)
    result = jnp.dot(ends, shift[...], preferred_element_type=F32)
    shear_lr[0] = result[:DEPTH]
    shear_lr[ROWS + 1] = result[DEPTH:]

    for o in range(1, nx):
        one(o, gx).wait_send()
        one(o, lax.rem(gx + nx - o, nx)).wait_recv()
    joined = parts[0]
    for i in range(1, nx):
        joined = joined + parts[i]
    coarse[gy] = joined
    for o in range(1, ny):
        two(o, gy).start()
    def first_sweep(p):
        m = shear[p + 1, 8:24, :]
        mu, md = shear[p, 8:24, :], shear[p + 2, 8:24, :]
        mo, mb = shear[p + 1, 7:23, :], shear[p + 1, 9:25, :]
        ml, mr = shear_lr[p, :, :LANES], shear_lr[p, :, LANES:]
        diag = MASS_TERM + 3.0 * m + 0.5 * ((mu + md) + (ml + mr) + (mo + mb))
        cut = 0.5 * jnp.where(lane == 7, m - mr, jnp.where(lane == 120, m - ml, 0.0))
        return m, mu, md, ml, mr, diag, cut

    ratio = 1.0 / RELAX_WEIGHT
    for p, side in ((0, 0), (ROWS + 1, 1)):
        _, _, _, _, _, diag, cut = first_sweep(p)
        end_s[side] = RELAX_WEIGHT / diag
        q1[p, 8:24, :] = diag / (diag + cut)

    def sweep_block(s, _):
        for q in range(SX):
            r = s * SX + q
            m, mu, md, ml, mr, diag, cut = first_sweep(r + 1)
            gl[r] = m + ml
            gr[r] = m + mr
            scale = RELAX_WEIGHT / diag
            cut_scale = RELAX_WEIGHT / (diag + cut)
            ratio_diag = ratio * diag
            s0[r] = scale
            s1[r] = cut_scale
            q1[r + 1, 8:24, :] = cut_scale * ratio_diag
            x = scale * b_t[:, r]
            x0[:, r + 1, 8:24, :] = x
            lhs[r, :, :, :LANES] = x.astype(BF16)
            if q in (7, 8):
                e = s * 2 + (q - 7)
                diag = diag + 0.5 * (m - (md if q == 7 else mu))
                for v, dg in ((0, diag), (1, diag + cut)):
                    scale = RELAX_WEIGHT / dg
                    sr[v, e] = scale
                    qr[v, e, 8:24, :] = scale * ratio_diag
        return 0

    lax.fori_loop(0, SUBS, sweep_block, 0)
    for v in range(2):
        rows = []
        for e in range(2 * SUBS):
            r = (e // 2) * SX + 7 + e % 2
            theirs = jnp.where(pair == 2 * (r & 31), edge_q[r // 32], 0.0)
            rows.append(jnp.concatenate([qr[v, e, 8:24, :], theirs], axis=1))
        rows = jnp.concatenate(rows, axis=0).astype(BF16)
        result = jnp.dot(rows, shift[...], preferred_element_type=F32)
        qr_lr[v] = result.reshape(2 * SUBS, DEPTH, 2 * LANES)

    for copy in halos_b:
        copy.wait()
    for side, p, keep in ((0, 0, k_up), (1, ROWS + 1, k_down)):
        x0[:, p, 8:24, :] = end_s[side] * (rows_got[side, 2:5] * keep)
    for h in range(2):
        for c in range(COMPS):
            edge_x[h, c] = edge_s[h] * joined_edge(2 + 2 * c + h)

    def sweep_edges(i, _):
        for j in range(8):
            r = i * 8 + j
            here = pair == 2 * (r & 31)
            lhs[r, :, :, LANES:] = jnp.where(here, edge_x[i // 4], 0.0).astype(BF16)
        return 0

    lax.fori_loop(0, ROWS // 8, sweep_edges, 0)

    edge_lo, edge_hi = lane < 8, lane >= 120
    w0 = jnp.where(edge_lo | edge_hi, 0.25, 0.5).astype(F32)
    w1 = jnp.where(edge_lo, 0.25 * k_left, jnp.where(edge_hi, 0.25 * k_right, 0.0)).astype(F32)
    few = 4

    def second_block(s, _):
        for j in range(SX // few):
            rows = lhs[pl.ds(s * SX + j * few, few)].reshape(few * COMPS * DEPTH, 2 * LANES)
            result = jnp.dot(rows, shift[...], preferred_element_type=F32)
            moved[j * few : (j + 1) * few] = result.reshape(few, COMPS, DEPTH, 2 * LANES)
        for q in range(SX):
            r = s * SX + q
            m = shear[r + 2, 8:24, :]
            gu, gd = m + shear[r + 1, 8:24, :], m + shear[r + 3, 8:24, :]
            go, gb = m + shear[r + 2, 7:23, :], m + shear[r + 2, 9:25, :]
            g_l, g_r = gl[r], gr[r]
            if q < 8:
                keep = jnp.where((gx == 0) & (s == 0), 0.5, 1.0)
            else:
                keep = jnp.where((gx == nx - 1) & (s == SUBS - 1), 0.5, 1.0)
            rest = keep - 0.5
            a0, a1 = w0 * s0[r], w1 * s1[r]
            qu, qd = q1[r, 8:24, :], q1[r + 2, 8:24, :]
            qo, qb = q1[r + 1, 7:23, :], q1[r + 1, 9:25, :]
            qm = q1[r + 1, 8:24, :]
            ql = jnp.where(lane == 121, pltpu.roll(qm, 1, 1), 1.0)
            ql = jnp.where(lane == 120, 0.0, ql)
            qn = jnp.where(lane == 6, pltpu.roll(qm, LANES - 1, 1), 1.0)
            qn = jnp.where(lane == 7, 0.0, qn)
            e = s * 2 + (0 if q < 8 else 1)
            if q in (7, 8):
                r0, r1 = rest * w0 * sr[0, e], rest * w1 * sr[1, e]
                a0, a1 = 0.5 * a0, 0.5 * a1
                ca = a0 + a1 + r0 + r1
                cu = (a0 + r0) + (a1 + r1) * qu if q == 7 else a0 + a1 * qu
                cd = (a0 + r0) + (a1 + r1) * qd if q == 8 else a0 + a1 * qd
                co = (a0 + a1 * qo) + (r0 * qr[0, e, 7:23, :] + r1 * qr[1, e, 7:23, :])
                cb = (a0 + a1 * qb) + (r0 * qr[0, e, 9:25, :] + r1 * qr[1, e, 9:25, :])
                r1l, r1r = jnp.where(lane == 120, 0.0, r1), jnp.where(lane == 7, 0.0, r1)
                cl = (a0 + a1 * ql) + (r0 * qr_lr[0, e, :, :LANES] + r1l * qr_lr[1, e, :, :LANES])
                cr = (a0 + a1 * qn) + (r0 * qr_lr[0, e, :, LANES:] + r1r * qr_lr[1, e, :, LANES:])
            else:
                if q in (6, 9):
                    k0 = 0.5 + rest * qr[0, e, 8:24, :]
                    near = a0 * k0
                    qx = qd if q == 6 else qu
                    near = near + a1 * (0.5 * qx + rest * qr[1, e, 8:24, :])
                a0, a1 = keep * a0, keep * a1
                ca = a0 + a1
                cu = near if q == 9 else a0 + a1 * qu
                cd = near if q == 6 else a0 + a1 * qd
                co = a0 + a1 * qo
                cb = a0 + a1 * qb
                cl = a0 + a1 * ql
                cr = a0 + a1 * qn
            ca = 2.4 * ca
            cu, cd, co, cb, cl, cr = cu * gu, cd * gd, co * go, cb * gb, cl * g_l, cr * g_r
            for c in range(COMPS):
                total = ca * b_t[c, r] + cu * x0[c, r, 8:24, :]
                total = total + (cd * x0[c, r + 2, 8:24, :] + co * x0[c, r + 1, 7:23, :])
                total = total + (cb * x0[c, r + 1, 9:25, :] + cl * moved[q, c, :, :LANES])
                loc_t[c, r] = total + cr * moved[q, c, :, LANES:]
        part = pl.ds(s * SX, SX)
        for d in range(DEPTH):
            pltpu.make_async_copy(
                loc_t.at[:, part, d, :], loc_n.at[:, d, part, :], loc_sem
            ).start()
        return 0


    lax.fori_loop(0, SUBS, second_block, 0)

    pltpu.make_async_copy(pieces, pieces, g_sem).wait()
    for o in range(1, ny):
        two(o, gy).wait_send()
        two(o, lax.rem(gy + ny - o, ny)).wait_recv()
    for s in range(SUBS):
        fetched = jnp.zeros((KMAX, LANES), F32)
        for l in range(NLIST):
            n = table_ref[s, 0, l]
            tile = jnp.where(lane8 == (n >> 4), coarse[n & (ny - 1)], 0.0)
            fetched = jnp.where(lane8 == l, jnp.sum(tile, axis=1, keepdims=True), fetched)
        acc = jnp.zeros((KMAX, NLIST), F32)
        for b in range(KMAX):
            acc = acc + pieces[s, b] * fetched[b : b + 1, :NLIST]
        answer = jnp.broadcast_to(jnp.sum(acc, axis=1, keepdims=True), (KMAX, LANES))
        answer = jnp.where(sub8 < tally_ref[0, s], answer, 0.0)
        sol[s] = answer.astype(BF16).astype(F32)
    pltpu.make_async_copy(loc_n, loc_n, loc_sem).wait()


def finish(loc_n, v_n, sol, out_hbm, out_v, out_sem):
    def out_copy(s):
        part = pl.ds(s * SX, SX)
        return pltpu.make_async_copy(out_v.at[:, :, part], out_hbm.at[:, :, part], out_sem.at[s])

    for s in range(SUBS):
        part = slice(s * SX, s * SX + SX)
        weights = [jnp.broadcast_to(sol[s, k : k + 1, :], (SX, LANES)) for k in range(KMAX)]

        def prolong(i, _):
            for j in range(4):
                d = i * 4 + j
                for c in range(COMPS):
                    total = loc_n[c, d, part, :]
                    for k in range(KMAX):
                        total = total + v_n[k, c, d, part, :].astype(F32) * weights[k]
                    out_v[c, d, part, :] = total
            return 0

        lax.fori_loop(0, DEPTH // 4, prolong, 0)
        out_copy(s).start()
    for s in range(SUBS):
        out_copy(s).wait()


def local(
    equation_misfit,
    thermal_excess,
    spanning_vectors,
    global_solve_pieces,
    influencing_partition_table,
    spanning_vector_tally,
):
    nx, ny = lax.axis_size("gx"), lax.axis_size("gy")
    hbm = pl.BlockSpec(memory_space=pltpu.HBM)
    smem = pl.BlockSpec(memory_space=pltpu.SMEM)
    vmem = pl.BlockSpec(memory_space=pltpu.VMEM)
    plane = (DEPTH, LANES)
    wide = (DEPTH, 2 * LANES)
    cuts = 2 * SUBS

    def f32(*shape):
        return pltpu.VMEM(shape, F32)

    def low(*shape):
        return pltpu.VMEM(shape, BF16)

    dma = pltpu.SemaphoreType.DMA
    scratch = [
        f32(ROWS, *plane),
        f32(COMPS, ROWS, *plane),
        f32(COMPS, DEPTH, ROWS, LANES),
        f32(SUBS, KMAX, KMAX, NLIST),
        f32(ROWS + 4, 32, LANES),
        f32(ROWS + 2, *wide),
        f32(8, *plane),
        f32(2, 8, *plane),
        f32(2, 5, *plane),
        f32(2, 5, *plane),
        f32(4, *plane),
        f32(2, *plane),
        f32(2, COMPS, *plane),
        f32(2, *plane),
        f32(2, *plane),
        f32(2, *plane),
        low(2 * LANES, 2 * LANES),
        f32(COMPS, ROWS + 2, 32, LANES),
        low(ROWS, COMPS, *wide),
        f32(SX, COMPS, *wide),
        f32(ROWS, *plane),
        f32(ROWS, *plane),
        f32(ROWS + 2, 32, LANES),
        f32(ROWS, *plane),
        f32(ROWS, *plane),
        f32(2, cuts, *plane),
        f32(2, cuts, 32, LANES),
        f32(2, cuts, *wide),
        f32(COMPS, ROWS, *plane),
        f32(SUBS, KMAX, SX, LANES),
        f32(nx, KMAX, LANES),
        f32(ny, KMAX, LANES),
        dma,
        dma,
        dma,
        dma,
        dma((2 * COMPS,)),
        dma,
        dma((12,)),
        dma((12,)),
        dma((nx - 1,)),
        dma((nx - 1,)),
        dma((ny - 1,)),
        dma((ny - 1,)),
    ]
    loc, vectors, sol = pl.pallas_call(
        kernel,
        out_shape=[
            pltpu.VMEM(equation_misfit.shape, F32),
            pltpu.VMEM(spanning_vectors.shape, BF16),
            pltpu.VMEM((SUBS, KMAX, LANES), F32),
        ],
        in_specs=[hbm, hbm, hbm, hbm, smem, smem],
        out_specs=[vmem] * 3,
        scratch_shapes=scratch,
        compiler_params=pltpu.CompilerParams(
            collective_id=0, has_side_effects=True, vmem_limit_bytes=52 * 2**20
        ),
        name="schwarz",
    )(
        equation_misfit,
        thermal_excess,
        spanning_vectors,
        jnp.transpose(global_solve_pieces, (0, 1, 3, 4, 2)),
        influencing_partition_table,
        jnp.transpose(spanning_vector_tally),
    )
    return pl.pallas_call(
        finish,
        out_shape=jax.ShapeDtypeStruct(equation_misfit.shape, F32),
        in_specs=[vmem] * 3,
        out_specs=hbm,
        scratch_shapes=[f32(COMPS, DEPTH, ROWS, LANES), dma((SUBS,))],
        compiler_params=pltpu.CompilerParams(vmem_limit_bytes=40 * 2**20),
        name="finish",
    )(loc, vectors, sol)


def solution(mesh):
    return jax.shard_map(
        local,
        mesh=mesh,
        in_specs=(
            P(None, None, "gx", "gy"),
            P(None, "gx", "gy"),
            P(None, None, None, "gx", "gy"),
            P("gx", "gy", None, None, None),
            P("gx", "gy", None),
            P("gx", "gy"),
        ),
        out_specs=P(None, None, "gx", "gy"),
        check_vma=False,
    )
```
